32 devices in a mesh: groups: 2 (over y), ctx: 4 (over z), head: 2 (over x), rep: 2 (over core).
Axes of the slice: x: 2, y: 2, z: 4, core: 2. Of those that a mesh axis runs over, the one named last changes fastest.
Arguments:
- queries: bfloat16 [2048, 8192], P(('groups', 'rep'), 'head'), parts along dimension 0, may hold values from -6 to 6
- cached_keys: bfloat16 [32768, 1024], P(('groups', 'ctx'), 'head'), parts along dimension 0, may hold values from -6 to 6
- cached_values: bfloat16 [32768, 1024], P(('groups', 'ctx'), 'head'), parts along dimension 0, may hold values from -6 to 6
- pattern: int32 [16, 16], P(('groups', 'rep')), parts along dimension 0, may hold values from 0 to 127, as said below
- out_weight: bfloat16 [8192, 8192], P('head', 'ctx'), may hold values from -1.1953125 to 1.1953125
Outputs:
- projected: bfloat16 [2048, 8192], P(('groups', 'rep'), ('ctx', 'head')), parts along dimension 0
The draws below stay inside these ranges and needn't reach their ends.
There are 2 independent parts, one for each index of `groups`. The reference program is written for one: setup_inputs(seed, part) draws one part's arguments, and reference() takes and returns one part's arrays. A program takes and returns all parts, laid end to end along the dimension named above; an argument that names none is the same for every part. Nothing has to cross between parts.
Inputs may be any that keep to these rules, and one draw needn't show every extreme that they name: Each row of pattern names 16 different key blocks; no row names more than 8 blocks among blocks k * 32 to (k + 1) * 32 - 1 for any k, and every row names exactly 8 in some such range.
All inputs are finite; a program needn't handle non-finite values.
Results may differ from the reference program's by a relative error of at most 0.0055.
Values may be sent and summed in bfloat16 or wider, within the bound.
A program may use at most 128 MiB of HBM per device.

```python
import jax
import jax.numpy as jnp
from jax import lax

D = 8192
HEADS = 64
KV_HEADS = 8
HEAD_DIM = 128
BLOCK = 128
KB_DEV = 32
QB = 8
Q_TOK = 1024
KBLOCKS = 128
TOPK = 16
CAP = 8
N_CTX = 4


def draw_queries(key, part):
    first_key = jax.random.fold_in(jax.random.fold_in(key, 3), 0)
    base = jnp.clip(5.0 * jax.random.normal(first_key, (Q_TOK, HEADS, HEAD_DIM), jnp.float32), -6.0, 6.0)
    return base.reshape(Q_TOK, HEADS * HEAD_DIM).astype(jnp.bfloat16)


def draw_cached_keys(key, part):
    total_rows = KBLOCKS * BLOCK
    first_key = jax.random.fold_in(jax.random.fold_in(key, 5), 0)
    base = jnp.clip(0.3 * jax.random.normal(first_key, (total_rows, KV_HEADS, HEAD_DIM), jnp.float32), -6.0, 6.0)
    return base.reshape(total_rows, KV_HEADS * HEAD_DIM).astype(jnp.bfloat16)


def draw_pattern(key, part):
    hot_key, slot_key, order_key = jax.random.split(jax.random.fold_in(key, 9), 3)
    hot_shard = jax.random.randint(hot_key, (QB, 1, 1), 0, N_CTX)
    shard_ids = jnp.arange(N_CTX, dtype=jnp.int32)[None, :, None]
    block_scores = jax.random.randint(order_key, (QB, N_CTX, KB_DEV), 0, 1 << 20) * KB_DEV + jnp.arange(KB_DEV, dtype=jnp.int32)[None, None, :]
    shuffled = jnp.argsort(block_scores, axis=-1).astype(jnp.int32)[:, :, :CAP]
    block_ids = shard_ids * KB_DEV + shuffled
    slot_draws = jax.random.randint(slot_key, (QB, N_CTX, CAP), 0, 1 << 16) + 1
    slot_rank = jnp.where(shard_ids == hot_shard, 0, slot_draws) * (N_CTX * CAP)
    slot_rank = slot_rank + jnp.arange(N_CTX * CAP, dtype=jnp.int32).reshape(1, N_CTX, CAP)
    picked = jnp.argsort(slot_rank.reshape(QB, N_CTX * CAP), axis=-1).astype(jnp.int32)[:, :TOPK]
    return jnp.take_along_axis(block_ids.reshape(QB, N_CTX * CAP), picked, axis=1).astype(jnp.int32)


def levels(key, extent, pieces, smallest, high):
    def one(dim, shards_of):
        heights = jax.random.uniform(jax.random.fold_in(jax.random.fold_in(key, 6), dim), (shards_of,), jnp.float32, smallest / len(pieces), high / len(pieces))
        return jnp.repeat(jnp.exp(heights), extent[dim] // shards_of).reshape((-1,) + (1,) * (len(extent) - dim - 1))

    loudness = one(*pieces[0])
    for cut in pieces[1:]:
        loudness = loudness * one(*cut)
    return loudness


def gaussian(rng, shape, spread, bound, cuts=(), kind=jnp.bfloat16):
    values = jax.random.normal(rng, shape, jnp.float32) * spread
    if len(cuts) > 0:
        values = levels(rng, shape, cuts, -0.22, 0.18) * values
    return jnp.clip(values, min=-bound, max=bound).astype(kind)


def setup_inputs(seed: int = 0, part: int = 0) -> dict:
    seeds = jax.random.split(jax.random.key(seed), 6)
    part_splits = jax.random.split(jax.random.fold_in(seeds[5], part), 6)
    queries = draw_queries(jax.random.fold_in(jax.random.fold_in(seeds[5], part), 71), part)
    cached_keys = draw_cached_keys(jax.random.fold_in(jax.random.fold_in(seeds[5], part), 71), part)
    cached_values = gaussian(part_splits[2], (KBLOCKS * BLOCK, KV_HEADS * HEAD_DIM), 1.0, 6.0, ((0, 4), (1, 2)))
    pattern = draw_pattern(jax.random.fold_in(jax.random.fold_in(seeds[5], part), 71), part)
    out_weight = gaussian(seeds[4], (HEADS * HEAD_DIM, D), 0.2, 1.1953125, ((0, 2), (1, 4)))
    return {"queries": queries, "cached_keys": cached_keys, "cached_values": cached_values, "pattern": pattern, "out_weight": out_weight}


def reference(queries, cached_keys, cached_values, pattern, out_weight):
    group_size = HEADS // KV_HEADS
    score_scale = HEAD_DIM ** -0.5
    key_blocks = cached_keys.reshape(KBLOCKS, BLOCK, KV_HEADS, HEAD_DIM)
    value_blocks = cached_values.reshape(KBLOCKS, BLOCK, KV_HEADS, HEAD_DIM)
    query_blocks = queries.reshape(QB, BLOCK, KV_HEADS, group_size, HEAD_DIM)
    segment_ids = jnp.arange(N_CTX, dtype=jnp.int32)

    def attend(inputs):
        query_block, chosen = inputs
        keys_sel = key_blocks[chosen].astype(jnp.float32)
        values_sel = value_blocks[chosen].astype(jnp.float32)
        scores = jnp.einsum('rkgd,tskd->kgrts', query_block.astype(jnp.float32), keys_sel) * score_scale
        block_top = scores.max(axis=-1)
        segment = (chosen // KB_DEV).astype(jnp.int32)
        member = segment[:, None] == segment_ids[None, :]
        seg_max = jnp.max(jnp.where(member, block_top[..., None], jnp.float32(-1e30)), axis=-2)
        key_max = jnp.take(seg_max, segment, axis=-1)
        shifted = jnp.exp(scores - key_max[..., None])
        probs = shifted.astype(jnp.bfloat16)
        block_total = shifted.sum(axis=-1)
        block_out = jnp.einsum('kgrts,tskd->kgrtd', probs.astype(jnp.float32), values_sel)
        row_max = seg_max.max(axis=-1)
        rescale = jnp.exp(key_max - row_max[..., None])
        numer = jnp.sum(block_out * rescale[..., None], axis=3)
        denom = jnp.sum(block_total * rescale, axis=3)
        result = numer / denom[..., None]
        return result.transpose(2, 0, 1, 3).reshape(BLOCK, HEADS * HEAD_DIM).astype(jnp.bfloat16)

    attended = lax.map(attend, (query_blocks, pattern)).reshape(Q_TOK, HEADS * HEAD_DIM)
    return jnp.dot(attended, out_weight, preferred_element_type=jnp.float32).astype(jnp.bfloat16)
```

```python
import functools
import math

import jax
import jax.numpy as jnp
from jax import lax
from jax.experimental import pallas as pl
from jax.experimental.pallas import tpu as pltpu
from jax.sharding import PartitionSpec as P

HEADS = 64
KV_HEADS = 8
HEAD_DIM = 128
BLOCK = 128
CAP = 8
UNIT_HEADS = 2
GROUP = HEADS // KV_HEADS
PAIRS = GROUP // (2 * UNIT_HEADS)
UNIT = UNIT_HEADS * HEAD_DIM
NEG = -1e30
MESH = pl.DeviceIdType.MESH


def kernel(n, exchange, slots, q_hbm, k_hbm, v_hbm, pat_ref, w_hbm, out_ref,
           q_ref, k_ref, v_ref, w_ref, idx_ref, cnt_ref, kg_ref, vg_ref,
           own_o, own_s, send_o, send_s, left_o, left_s, right_o, right_s, res,
           acc, keep, xs, xr,
           load_sem, so_sem, ss_sem, lo_sem, ls_sem, ro_sem, rs_sem,
           res_recv, res_left, res_right, xs_sem, xr_sem):
    c = lax.axis_index("ctx")
    h = lax.axis_index("head")
    q_blocks = q_ref.shape[0]
    heads_kv = k_ref.shape[2] // HEAD_DIM
    local_blocks = k_ref.shape[0]
    per_block = heads_kv * PAIRS
    total = q_blocks * per_block
    width = w_ref.shape[1]
    share = width // 2
    roots = (max(n // 2 - 1, 0), n // 2)

    loads = [
        pltpu.make_async_copy(src, dst, load_sem.at[i])
        for i, (src, dst) in enumerate(
            ((k_hbm, k_ref), (v_hbm, v_ref), (q_hbm, q_ref), (w_hbm, w_ref))
        )
    ]
    for load in loads:
        load.start()

    barrier = pltpu.get_barrier_semaphore()

    @pl.when(c > 0)
    def _():
        pl.semaphore_signal(barrier, inc=1, device_id={"ctx": c - 1}, device_id_type=MESH)

    @pl.when(c < n - 1)
    def _():
        pl.semaphore_signal(barrier, inc=1, device_id={"ctx": c + 1}, device_id_type=MESH)

    if exchange:
        pl.semaphore_signal(barrier, inc=1, device_id={"head": 1 - h}, device_id_type=MESH)

    for b in range(q_blocks):
        count = jnp.int32(0)
        packed = [jnp.int32(0)] * CAP
        for j in range(pat_ref.shape[1]):
            local = pat_ref[b, j] - c * local_blocks
            inside = (local >= 0) & (local < local_blocks)
            for s in range(CAP):
                packed[s] = jnp.where(inside & (count == s), local, packed[s])
            count = count + inside.astype(jnp.int32)
        for s in range(CAP):
            idx_ref[b, s] = packed[s]
        cnt_ref[b] = count

    pl.semaphore_wait(barrier, (c > 0).astype(jnp.int32) + (c < n - 1).astype(jnp.int32) + int(exchange))
    loads[0].wait()
    loads[1].wait()
    loads[2].wait()

    scale = HEAD_DIM ** (-0.5) * math.log2(math.e)

    def up_copies(u, a, right):
        dst_o, dst_s = (left_o, left_s) if right else (right_o, right_s)
        rec_o, rec_s = (lo_sem, ls_sem) if right else (ro_sem, rs_sem)
        to = {"ctx": c + 1} if right else {"ctx": c - 1}
        return (
            pltpu.make_async_remote_copy(
                send_o.at[u, a], dst_o.at[u, a], so_sem.at[u, a], rec_o.at[u, a],
                device_id=to, device_id_type=MESH),
            pltpu.make_async_remote_copy(
                send_s.at[u, a], dst_s.at[u, a], ss_sem.at[u, a], rec_s.at[u, a],
                device_id=to, device_id_type=MESH),
        )

    def down_copy(u, a, right):
        return pltpu.make_async_remote_copy(
            res.at[u, a], res.at[u, a], (res_right if right else res_left).at[u, a],
            res_recv.at[u, a],
            device_id={"ctx": c + 1} if right else {"ctx": c - 1}, device_id_type=MESH)

    def x_copy(b):
        return pltpu.make_async_remote_copy(
            xs.at[b], xr.at[b], xs_sem.at[b], xr_sem.at[b],
            device_id={"head": 1 - h}, device_id_type=MESH)

    def attend(u):
        b = u // per_block
        k = (u // PAIRS) % heads_kv
        slot = u % slots

        @pl.when(u % PAIRS == 0)
        def _():
            column = pl.ds(pl.multiple_of(k * HEAD_DIM, HEAD_DIM), HEAD_DIM)
            for s in range(CAP):
                chosen = idx_ref[b, s]
                kg_ref[s * BLOCK:(s + 1) * BLOCK, :] = k_ref[chosen, :, column]
                vg_ref[s * BLOCK:(s + 1) * BLOCK, :] = v_ref[chosen, :, column]

        count = cnt_ref[b]
        for a in range(2):
            column = pl.multiple_of(((u % per_block) * 2 + a) * UNIT, UNIT)
            q = q_ref[b, :, pl.ds(column, UNIT)]
            q = jnp.concatenate(
                [q[:, i * HEAD_DIM:(i + 1) * HEAD_DIM] for i in range(UNIT_HEADS)], axis=0)
            scores = lax.dot_general(
                kg_ref[...], q, (((1,), (1,)), ((), ())), preferred_element_type=jnp.float32)
            parts = []
            for s in range(CAP):
                live = s < count
                parts.append(
                    scores[s * BLOCK:(s + 1) * BLOCK] * jnp.where(live, scale, 0.0)
                    + jnp.where(live, 0.0, NEG))
            scores = jnp.concatenate(parts, axis=0)
            top = jnp.max(scores, axis=0, keepdims=True)
            weights = jnp.exp2(scores - jnp.maximum(top, 0.1 * NEG))
            norm = jnp.sum(weights, axis=0, keepdims=True)
            own_o[slot, a] = lax.dot_general(
                vg_ref[...], weights.astype(jnp.bfloat16), (((0,), (0,)), ((), ())),
                preferred_element_type=jnp.float32)
            for i in range(UNIT_HEADS):
                lanes = slice(i * HEAD_DIM, (i + 1) * HEAD_DIM)
                own_s[slot, a, i:i + 1, :] = top[:, lanes]
                own_s[slot, a, UNIT_HEADS + i:UNIT_HEADS + i + 1, :] = norm[:, lanes]

    def fold(slot, a, got_o, got_s):
        mine = own_s[slot, a]
        m1, l1 = mine[:UNIT_HEADS], mine[UNIT_HEADS:2 * UNIT_HEADS]
        m2, l2 = got_s[:UNIT_HEADS], got_s[UNIT_HEADS:2 * UNIT_HEADS]
        top = jnp.maximum(m1, m2)
        f1, f2 = jnp.exp2(m1 - top), jnp.exp2(m2 - top)
        for i in range(UNIT_HEADS):
            lanes = slice(i * HEAD_DIM, (i + 1) * HEAD_DIM)
            own_o[slot, a, :, lanes] = (
                own_o[slot, a, :, lanes] * f1[i:i + 1]
                + got_o[:, lanes].astype(jnp.float32) * f2[i:i + 1])
        own_s[slot, a, :UNIT_HEADS, :] = top
        own_s[slot, a, UNIT_HEADS:2 * UNIT_HEADS, :] = l1 * f1 + l2 * f2

    def merge(u, a):
        root = roots[a]
        slot = u % slots

        @pl.when((c > 0) & (c <= root))
        def _():
            for copy in up_copies(u, a, True):
                copy.wait_recv()
            fold(slot, a, left_o[u, a], left_s[u, a])

        @pl.when((c < n - 1) & (c >= root))
        def _():
            for copy in up_copies(u, a, False):
                copy.wait_recv()
            fold(slot, a, right_o[u, a], right_s[u, a])

        @pl.when(c != root)
        def _():
            send_o[u, a] = own_o[slot, a].astype(jnp.bfloat16)
            send_s[u, a] = own_s[slot, a]

        @pl.when(c < root)
        def _():
            for copy in up_copies(u, a, True):
                copy.start()

        @pl.when(c > root)
        def _():
            for copy in up_copies(u, a, False):
                copy.start()

        @pl.when(c == root)
        def _():
            norm = own_s[slot, a, UNIT_HEADS:2 * UNIT_HEADS, :]
            for i in range(UNIT_HEADS):
                lanes = slice(i * HEAD_DIM, (i + 1) * HEAD_DIM)
                done = own_o[slot, a, :, lanes] / norm[i:i + 1]
                res[u, a, :, lanes] = done.T.astype(jnp.bfloat16)
            spread(u, a)

    def spread(u, a):
        @pl.when((c > 0) & (c <= roots[a]))
        def _():
            down_copy(u, a, False).start()

        @pl.when((c < n - 1) & (c >= roots[a]))
        def _():
            down_copy(u, a, True).start()

    def receive(u, a):
        @pl.when(c != roots[a])
        def _():
            down_copy(u, a, True).wait_recv()
            spread(u, a)

    def project(u):
        b = u // per_block
        lhs = jnp.concatenate([res[u, 0], res[u, 1]], axis=1)
        rows = pl.ds(pl.multiple_of((u % per_block) * 2 * UNIT, 2 * UNIT), 2 * UNIT)
        product = jnp.dot(lhs, w_ref[rows, :], preferred_element_type=jnp.float32)

        @pl.when(u % per_block == 0)
        def _():
            acc[...] = product

        @pl.when(u % per_block != 0)
        def _():
            acc[...] += product

        @pl.when(u % per_block == per_block - 1)
        def _():
            if exchange:
                mine = pl.multiple_of(h * share, 128)
                other = pl.multiple_of((1 - h) * share, 128)
                xs[b] = acc[:, pl.ds(other, share)].astype(jnp.bfloat16)
                x_copy(b).start()
                keep[b] = acc[:, pl.ds(mine, share)]
            else:
                out_ref[b] = acc[...]

    def span(far, root):
        return jnp.where(c < root, c, jnp.where(c > root, n - 1 - c, far))

    far = [max(r, n - 1 - r) for r in roots]
    merge_lag = [span(f, r) for f, r in zip(far, roots)]
    result_lag = [f + jnp.abs(c - r) for f, r in zip(far, roots)]
    last_lag = jnp.maximum(result_lag[0], result_lag[1])
    steps = total + max(f + max(r, n - 1 - r) for f, r in zip(far, roots))

    def step(t, carry):
        @pl.when(t < total)
        def _():
            attend(t)

        for a in range(2):
            u = t - merge_lag[a]

            @pl.when((u >= 0) & (u < total))
            def _(u=u, a=a):
                merge(u, a)

        for a in range(2):
            u = t - result_lag[a]

            @pl.when((u >= 0) & (u < total))
            def _(u=u, a=a):
                receive(u, a)

        u = t - last_lag

        @pl.when(t == 0)
        def _():
            loads[3].wait()

        @pl.when((u >= 0) & (u < total))
        def _():
            project(u)

        return carry

    lax.fori_loop(0, steps, step, 0)

    if exchange:
        for b in range(q_blocks):
            x_copy(b).wait_recv()
            out_ref[b] = (keep[b] + xr[b].astype(jnp.float32)).astype(out_ref.dtype)
            x_copy(b).wait_send()

    def drain(u, carry):
        for a in range(2):
            root = roots[a]

            @pl.when(c != root)
            def _():
                for copy in up_copies(u, a, True):
                    copy.wait_send()

            @pl.when((c > 0) & (c <= root))
            def _():
                down_copy(u, a, False).wait_send()

            @pl.when((c < n - 1) & (c >= root))
            def _():
                down_copy(u, a, True).wait_send()

        return carry

    lax.fori_loop(0, total, drain, 0)


def shards(n, n_head, queries, cached_keys, cached_values, pattern, out_weight):
    query_count, query_width = queries.shape
    q_blocks = query_count // BLOCK
    heads_kv = cached_keys.shape[1] // HEAD_DIM
    total = q_blocks * heads_kv * PAIRS
    width = out_weight.shape[1]
    share = width // 2
    exchange = n_head == 2 and share % 128 == 0
    slots = n // 2 + 1
    bf16, f32 = jnp.bfloat16, jnp.float32
    if exchange:
        out_shape = jax.ShapeDtypeStruct((q_blocks, BLOCK, share), bf16)
        x_rows = q_blocks
    else:
        out_shape = jax.ShapeDtypeStruct((q_blocks, BLOCK, width), f32)
        x_rows, share = 1, 128
    units = (total, 2)
    cache_shape = (cached_keys.shape[0] // BLOCK, BLOCK, cached_keys.shape[1])
    sem = pltpu.SemaphoreType.DMA
    any_space = pl.BlockSpec(memory_space=pl.ANY)
    out = pl.pallas_call(
        functools.partial(kernel, n, exchange, slots),
        out_shape=out_shape,
        in_specs=[any_space, any_space, any_space,
                  pl.BlockSpec(memory_space=pltpu.SMEM), any_space],
        out_specs=pl.BlockSpec(memory_space=pltpu.VMEM),
        scratch_shapes=[
            pltpu.VMEM((q_blocks, BLOCK, query_width), bf16),
            pltpu.VMEM(cache_shape, bf16),
            pltpu.VMEM(cache_shape, bf16),
            pltpu.VMEM(out_weight.shape, bf16),
            pltpu.SMEM((q_blocks, CAP), jnp.int32),
            pltpu.SMEM((q_blocks,), jnp.int32),
            pltpu.VMEM((CAP * BLOCK, HEAD_DIM), bf16),
            pltpu.VMEM((CAP * BLOCK, HEAD_DIM), bf16),
            pltpu.VMEM((slots, 2, HEAD_DIM, UNIT), f32),
            pltpu.VMEM((slots, 2, 8, BLOCK), f32),
            pltpu.VMEM(units + (HEAD_DIM, UNIT), bf16),
            pltpu.VMEM(units + (8, BLOCK), f32),
            pltpu.VMEM(units + (HEAD_DIM, UNIT), bf16),
            pltpu.VMEM(units + (8, BLOCK), f32),
            pltpu.VMEM(units + (HEAD_DIM, UNIT), bf16),
            pltpu.VMEM(units + (8, BLOCK), f32),
            pltpu.VMEM(units + (BLOCK, UNIT), bf16),
            pltpu.VMEM((BLOCK, width), f32),
            pltpu.VMEM((x_rows, BLOCK, share), f32),
            pltpu.VMEM((x_rows, BLOCK, share), bf16),
            pltpu.VMEM((x_rows, BLOCK, share), bf16),
            sem((4,)),
            sem(units), sem(units), sem(units), sem(units), sem(units), sem(units),
            sem(units), sem(units), sem(units),
            sem((x_rows,)), sem((x_rows,)),
        ],
        compiler_params=pltpu.CompilerParams(
            collective_id=0, has_side_effects=True, vmem_limit_bytes=60 * 1024 * 1024),
        cost_estimate=pl.CostEstimate(
            flops=4 * query_count * query_width * CAP * BLOCK
            + 2 * query_count * query_width * width,
            bytes_accessed=2 * (queries.size + 2 * cached_keys.size + out_weight.size),
            transcendentals=query_count * query_width * CAP),
    )(
        queries.reshape(q_blocks, BLOCK, query_width),
        cached_keys.reshape(cache_shape), cached_values.reshape(cache_shape), pattern, out_weight,
    )
    out = out.reshape(query_count, -1)
    if exchange:
        return out
    return lax.psum_scatter(out, "head", scatter_dimension=1, tiled=True).astype(bf16)


def solution(mesh):
    return jax.shard_map(
        functools.partial(shards, mesh.shape["ctx"], mesh.shape["head"]),
        mesh=mesh,
        in_specs=(
            P(("groups", "rep"), "head"),
            P(("groups", "ctx"), "head"),
            P(("groups", "ctx"), "head"),
            P(("groups", "rep"), None),
            P("head", "ctx"),
        ),
        out_specs=P(("groups", "rep"), ("ctx", "head")),
        check_vma=False,
    )
```

```python
import functools
import math

import jax
import jax.numpy as jnp
from jax import lax
from jax.experimental import pallas as pl
from jax.experimental.pallas import tpu as pltpu
from jax.sharding import PartitionSpec as P

HEADS = 64
KV_HEADS = 8
HEAD_DIM = 128
BLOCK = 128
CAP = 8
UNIT_HEADS = 2
GROUP = HEADS // KV_HEADS
PAIRS = GROUP // (2 * UNIT_HEADS)
UNIT = UNIT_HEADS * HEAD_DIM
NEG = -1e30
HOP = 2
MESH = pl.DeviceIdType.MESH


def kernel(n, exchange, slots, q_hbm, k_hbm, v_hbm, pat_ref, w_hbm, out_ref,
           q_ref, k_ref, v_ref, w_ref, idx_ref, cnt_ref, kg_ref, vg_ref,
           own_o, own_s, send_o, send_s, left_o, left_s, right_o, right_s, res,
           acc, keep, xs, xr,
           cache_sem, q_sem, w_sem, so_sem, ss_sem, lo_sem, ls_sem, ro_sem, rs_sem,
           res_recv, res_left, res_right, xs_sem, xr_sem):
    c = lax.axis_index("ctx")
    h = lax.axis_index("head")
    q_blocks = q_ref.shape[0]
    heads_kv = k_ref.shape[2] // HEAD_DIM
    local_blocks = k_ref.shape[0]
    per_block = heads_kv * PAIRS
    total = q_blocks * per_block
    width = w_ref.shape[1]
    share = width // 2
    roots = (max(n // 2 - 1, 0), n // 2)

    cache_loads = (
        pltpu.make_async_copy(k_hbm, k_ref, cache_sem.at[0]),
        pltpu.make_async_copy(v_hbm, v_ref, cache_sem.at[1]),
    )

    def load_queries(b):
        return pltpu.make_async_copy(q_hbm.at[b], q_ref.at[b], q_sem.at[b])

    def load_weights(k):
        rows = pl.ds(pl.multiple_of(k * GROUP * HEAD_DIM, GROUP * HEAD_DIM), GROUP * HEAD_DIM)
        return pltpu.make_async_copy(w_hbm.at[rows], w_ref.at[rows], w_sem.at[k])

    load_queries(0).start()
    for load in cache_loads:
        load.start()
    for b in range(1, q_blocks):
        load_queries(b).start()
    for k in range(heads_kv):
        load_weights(k).start()
    acc[...] = jnp.zeros_like(acc)

    barrier = pltpu.get_barrier_semaphore()

    @pl.when(c > 0)
    def _():
        pl.semaphore_signal(barrier, inc=1, device_id={"ctx": c - 1}, device_id_type=MESH)

    @pl.when(c < n - 1)
    def _():
        pl.semaphore_signal(barrier, inc=1, device_id={"ctx": c + 1}, device_id_type=MESH)

    if exchange:
        pl.semaphore_signal(barrier, inc=1, device_id={"head": 1 - h}, device_id_type=MESH)

    for b in range(q_blocks):
        count = jnp.int32(0)
        packed = [jnp.int32(0)] * CAP
        for j in range(pat_ref.shape[1]):
            local = pat_ref[b, j] - c * local_blocks
            inside = (local >= 0) & (local < local_blocks)
            for s in range(CAP):
                packed[s] = jnp.where(inside & (count == s), local, packed[s])
            count = count + inside.astype(jnp.int32)
        for s in range(CAP):
            idx_ref[b, s] = packed[s]
        cnt_ref[b] = count

    pl.semaphore_wait(barrier, (c > 0).astype(jnp.int32) + (c < n - 1).astype(jnp.int32) + int(exchange))

    for load in cache_loads:
        load.wait()

    scale = HEAD_DIM ** (-0.5) * math.log2(math.e)

    def up_copies(u, a, right):
        dst_o, dst_s = (left_o, left_s) if right else (right_o, right_s)
        rec_o, rec_s = (lo_sem, ls_sem) if right else (ro_sem, rs_sem)
        to = {"ctx": c + 1} if right else {"ctx": c - 1}
        return (
            pltpu.make_async_remote_copy(
                send_o.at[u, a], dst_o.at[u, a], so_sem.at[u, a], rec_o.at[u, a],
                device_id=to, device_id_type=MESH),
            pltpu.make_async_remote_copy(
                send_s.at[u, a], dst_s.at[u, a], ss_sem.at[u, a], rec_s.at[u, a],
                device_id=to, device_id_type=MESH),
        )

    def down_copy(u, a, right):
        return pltpu.make_async_remote_copy(
            res.at[u, a], res.at[u, a], (res_right if right else res_left).at[u, a],
            res_recv.at[u, a],
            device_id={"ctx": c + 1} if right else {"ctx": c - 1}, device_id_type=MESH)

    def x_copy(b):
        return pltpu.make_async_remote_copy(
            xs.at[b], xr.at[b], xs_sem.at[b], xr_sem.at[b],
            device_id={"head": 1 - h}, device_id_type=MESH)

    def attend(u):
        b = u // per_block
        k = (u // PAIRS) % heads_kv
        slot = u % slots

        @pl.when(u % per_block == 0)
        def _():
            load_queries(b).wait()

        @pl.when(u % PAIRS == 0)
        def _():
            column = pl.ds(pl.multiple_of(k * HEAD_DIM, HEAD_DIM), HEAD_DIM)
            for s in range(CAP):
                chosen = idx_ref[b, s]
                kg_ref[s * BLOCK:(s + 1) * BLOCK, :] = k_ref[chosen, :, column]
                vg_ref[:, s * BLOCK:(s + 1) * BLOCK] = v_ref[chosen, :, column].T

        count = cnt_ref[b]
        for a in range(2):
            column = pl.multiple_of(((u % per_block) * 2 + a) * UNIT, UNIT)
            q = q_ref[b, :, pl.ds(column, UNIT)]
            q = jnp.concatenate(
                [q[:, i * HEAD_DIM:(i + 1) * HEAD_DIM] for i in range(UNIT_HEADS)], axis=0)
            scores = lax.dot_general(
                kg_ref[...], q, (((1,), (1,)), ((), ())), preferred_element_type=jnp.float32)
            slabs = [scores[s * BLOCK:(s + 1) * BLOCK] for s in range(CAP)]
            top = jnp.full((1, UNIT), NEG, jnp.float32)
            for s, slab in enumerate(slabs):
                peak = jnp.max(slab, axis=0, keepdims=True) * scale
                top = jnp.maximum(top, jnp.where(s < count, peak, NEG))
            weights, norm = [], jnp.zeros((1, UNIT), jnp.float32)
            for s, slab in enumerate(slabs):
                weight = jnp.exp2(slab * scale - jnp.where(s < count, top, -NEG))
                norm = norm + jnp.sum(weight, axis=0, keepdims=True)
                weights.append(weight.astype(jnp.bfloat16))
            own_o[slot, a] = jnp.dot(
                vg_ref[...], jnp.concatenate(weights, axis=0),
                preferred_element_type=jnp.float32)
            for i in range(UNIT_HEADS):
                lanes = slice(i * HEAD_DIM, (i + 1) * HEAD_DIM)
                own_s[slot, a, i:i + 1, :] = top[:, lanes]
                own_s[slot, a, UNIT_HEADS + i:UNIT_HEADS + i + 1, :] = norm[:, lanes]

    def fold(slot, a, got_o, got_s):
        mine = own_s[slot, a]
        m1, l1 = mine[:UNIT_HEADS], mine[UNIT_HEADS:2 * UNIT_HEADS]
        m2, l2 = got_s[:UNIT_HEADS], got_s[UNIT_HEADS:2 * UNIT_HEADS]
        top = jnp.maximum(m1, m2)
        f1, f2 = jnp.exp2(m1 - top), jnp.exp2(m2 - top)
        for i in range(UNIT_HEADS):
            lanes = slice(i * HEAD_DIM, (i + 1) * HEAD_DIM)
            own_o[slot, a, :, lanes] = (
                own_o[slot, a, :, lanes] * f1[i:i + 1]
                + got_o[:, lanes].astype(jnp.float32) * f2[i:i + 1])
        own_s[slot, a, :UNIT_HEADS, :] = top
        own_s[slot, a, UNIT_HEADS:2 * UNIT_HEADS, :] = l1 * f1 + l2 * f2

    def merge(u, a):
        root = roots[a]
        slot = u % slots

        @pl.when((c > 0) & (c <= root))
        def _():
            for copy in up_copies(u, a, True):
                copy.wait_recv()
            fold(slot, a, left_o[u, a], left_s[u, a])

        @pl.when((c < n - 1) & (c >= root))
        def _():
            for copy in up_copies(u, a, False):
                copy.wait_recv()
            fold(slot, a, right_o[u, a], right_s[u, a])

        @pl.when(c != root)
        def _():
            send_o[u, a] = own_o[slot, a].astype(jnp.bfloat16)
            send_s[u, a] = own_s[slot, a]

        @pl.when(c < root)
        def _():
            for copy in up_copies(u, a, True):
                copy.start()

        @pl.when(c > root)
        def _():
            for copy in up_copies(u, a, False):
                copy.start()

        @pl.when(c == root)
        def _():
            norm = own_s[slot, a, UNIT_HEADS:2 * UNIT_HEADS, :]
            for i in range(UNIT_HEADS):
                lanes = slice(i * HEAD_DIM, (i + 1) * HEAD_DIM)
                done = own_o[slot, a, :, lanes] / norm[i:i + 1]
                res[u, a, :, lanes] = done.T.astype(jnp.bfloat16)
            spread(u, a)

    def spread(u, a):
        @pl.when((c > 0) & (c <= roots[a]))
        def _():
            down_copy(u, a, False).start()

        @pl.when((c < n - 1) & (c >= roots[a]))
        def _():
            down_copy(u, a, True).start()

    def receive(u, a):
        @pl.when(c != roots[a])
        def _():
            down_copy(u, a, True).wait_recv()
            spread(u, a)

    def finish(b):
        x_copy(b).wait_recv()
        out_ref[b] = (keep[b] + xr[b].astype(jnp.float32)).astype(out_ref.dtype)

    def project(u):
        b = u // per_block
        k = (u // PAIRS) % heads_kv

        @pl.when(u < per_block)
        def _():
            load_weights(k).wait()

        lhs = jnp.concatenate(
            [res[u - PAIRS + 1 + i, a] for i in range(PAIRS) for a in range(2)], axis=1)
        rows = pl.ds(pl.multiple_of(k * GROUP * HEAD_DIM, GROUP * HEAD_DIM), GROUP * HEAD_DIM)
        tile = min(width, 512)
        for start in range(0, width, tile):
            lanes = slice(start, start + tile)
            acc[:, lanes] += jnp.dot(lhs, w_ref[rows, lanes], preferred_element_type=jnp.float32)

        @pl.when(u % per_block == per_block - 1)
        def _():
            if exchange:
                mine = pl.multiple_of(h * share, 128)
                other = pl.multiple_of((1 - h) * share, 128)
                xs[b] = acc[:, pl.ds(other, share)].astype(jnp.bfloat16)
                x_copy(b).start()
                keep[b] = acc[:, pl.ds(mine, share)]

                @pl.when(b > 0)
                def _():
                    finish(b - 1)
            else:
                out_ref[b] = acc[...]
            acc[...] = jnp.zeros_like(acc)

    def span(far, root):
        return jnp.where(c < root, c, jnp.where(c > root, n - 1 - c, far))

    far = [max(r, n - 1 - r) for r in roots]
    merge_lag = [HOP * span(f, r) for f, r in zip(far, roots)]
    result_lag = [HOP * (f + jnp.abs(c - r)) for f, r in zip(far, roots)]
    last_lag = jnp.maximum(result_lag[0], result_lag[1])
    steps = total + HOP * max(f + max(r, n - 1 - r) for f, r in zip(far, roots))

    def step(t, carry):
        @pl.when(t < total)
        def _():
            attend(t)

        for a in range(2):
            u = t - merge_lag[a]

            @pl.when((u >= 0) & (u < total))
            def _(u=u, a=a):
                merge(u, a)

        for a in range(2):
            u = t - result_lag[a]

            @pl.when((u >= 0) & (u < total))
            def _(u=u, a=a):
                receive(u, a)

        u = t - last_lag

        @pl.when((u >= 0) & (u < total) & (u % PAIRS == PAIRS - 1))
        def _():
            project(u)

        return carry

    lax.fori_loop(0, steps, step, 0)

    if exchange:
        finish(q_blocks - 1)
        for b in range(q_blocks):
            x_copy(b).wait_send()

    def drain(u, carry):
        for a in range(2):
            root = roots[a]

            @pl.when(c != root)
            def _():
                for copy in up_copies(u, a, True):
                    copy.wait_send()

            @pl.when((c > 0) & (c <= root))
            def _():
                down_copy(u, a, False).wait_send()

            @pl.when((c < n - 1) & (c >= root))
            def _():
                down_copy(u, a, True).wait_send()

        return carry

    lax.fori_loop(0, total, drain, 0)


def shards(n, n_head, queries, cached_keys, cached_values, pattern, out_weight):
    query_count, query_width = queries.shape
    q_blocks = query_count // BLOCK
    heads_kv = cached_keys.shape[1] // HEAD_DIM
    total = q_blocks * heads_kv * PAIRS
    width = out_weight.shape[1]
    share = width // 2
    exchange = n_head == 2 and share % 128 == 0
    slots = HOP * (n // 2) + 1
    bf16, f32 = jnp.bfloat16, jnp.float32
    if exchange:
        out_shape = jax.ShapeDtypeStruct((q_blocks, BLOCK, share), bf16)
        x_rows = q_blocks
    else:
        out_shape = jax.ShapeDtypeStruct((q_blocks, BLOCK, width), f32)
        x_rows, share = 1, 128
    units = (total, 2)
    cache_shape = (cached_keys.shape[0] // BLOCK, BLOCK, cached_keys.shape[1])
    sem = pltpu.SemaphoreType.DMA
    any_space = pl.BlockSpec(memory_space=pl.ANY)
    out = pl.pallas_call(
        functools.partial(kernel, n, exchange, slots),
        out_shape=out_shape,
        in_specs=[any_space, any_space, any_space,
                  pl.BlockSpec(memory_space=pltpu.SMEM), any_space],
        out_specs=pl.BlockSpec(memory_space=pltpu.VMEM),
        scratch_shapes=[
            pltpu.VMEM((q_blocks, BLOCK, query_width), bf16),
            pltpu.VMEM(cache_shape, bf16),
            pltpu.VMEM(cache_shape, bf16),
            pltpu.VMEM(out_weight.shape, bf16),
            pltpu.SMEM((q_blocks, CAP), jnp.int32),
            pltpu.SMEM((q_blocks,), jnp.int32),
            pltpu.VMEM((CAP * BLOCK, HEAD_DIM), bf16),
            pltpu.VMEM((HEAD_DIM, CAP * BLOCK), bf16),
            pltpu.VMEM((slots, 2, HEAD_DIM, UNIT), f32),
            pltpu.VMEM((slots, 2, 8, BLOCK), f32),
            pltpu.VMEM(units + (HEAD_DIM, UNIT), bf16),
            pltpu.VMEM(units + (8, BLOCK), f32),
            pltpu.VMEM(units + (HEAD_DIM, UNIT), bf16),
            pltpu.VMEM(units + (8, BLOCK), f32),
            pltpu.VMEM(units + (HEAD_DIM, UNIT), bf16),
            pltpu.VMEM(units + (8, BLOCK), f32),
            pltpu.VMEM(units + (BLOCK, UNIT), bf16),
            pltpu.VMEM((BLOCK, width), f32),
            pltpu.VMEM((x_rows, BLOCK, share), f32),
            pltpu.VMEM((x_rows, BLOCK, share), bf16),
            pltpu.VMEM((x_rows, BLOCK, share), bf16),
            sem((2,)), sem((q_blocks,)), sem((heads_kv,)),
            sem(units), sem(units), sem(units), sem(units), sem(units), sem(units),
            sem(units), sem(units), sem(units),
            sem((x_rows,)), sem((x_rows,)),
        ],
        compiler_params=pltpu.CompilerParams(
            collective_id=0, has_side_effects=True, vmem_limit_bytes=60 * 1024 * 1024),
        cost_estimate=pl.CostEstimate(
            flops=4 * query_count * query_width * CAP * BLOCK
            + 2 * query_count * query_width * width,
            bytes_accessed=2 * (queries.size + 2 * cached_keys.size + out_weight.size),
            transcendentals=query_count * query_width * CAP),
    )(
        queries.reshape(q_blocks, BLOCK, query_width),
        cached_keys.reshape(cache_shape), cached_values.reshape(cache_shape), pattern, out_weight,
    )
    out = out.reshape(query_count, -1)
    if exchange:
        return out
    return lax.psum_scatter(out, "head", scatter_dimension=1, tiled=True).astype(bf16)


def solution(mesh):
    return jax.shard_map(
        functools.partial(shards, mesh.shape["ctx"], mesh.shape["head"]),
        mesh=mesh,
        in_specs=(
            P(("groups", "rep"), "head"),
            P(("groups", "ctx"), "head"),
            P(("groups", "ctx"), "head"),
            P(("groups", "rep"), None),
            P("head", "ctx"),
        ),
        out_specs=P(("groups", "rep"), ("ctx", "head")),
        check_vma=False,
    )
```

```python
import functools
import math

import jax
import jax.numpy as jnp
from jax import lax
from jax.experimental import pallas as pl
from jax.experimental.pallas import tpu as pltpu
from jax.sharding import PartitionSpec as P

HEADS = 64
KV_HEADS = 8
HEAD_DIM = 128
BLOCK = 128
CAP = 8
UNIT_HEADS = 4
GROUP = HEADS // KV_HEADS
PAIRS = GROUP // (2 * UNIT_HEADS)
UNIT = UNIT_HEADS * HEAD_DIM
NEG = -1e30
HOP = 2
MESH = pl.DeviceIdType.MESH


def kernel(n, exchange, slots, q_hbm, k_hbm, v_hbm, pat_ref, w_hbm, out_ref,
           q_ref, k_ref, v_ref, w_ref, idx_ref, cnt_ref, kg_ref, vg_ref,
           own_o, own_s, send_o, send_s, left_o, left_s, right_o, right_s, res,
           acc, keep, xs, xr,
           cache_sem, q_sem, w_sem, so_sem, ss_sem, lo_sem, ls_sem, ro_sem, rs_sem,
           res_recv, res_left, res_right, xs_sem, xr_sem):
    c = lax.axis_index("ctx")
    h = lax.axis_index("head")
    q_blocks = q_ref.shape[0]
    heads_kv = k_ref.shape[2] // HEAD_DIM
    local_blocks = k_ref.shape[0]
    per_block = heads_kv * PAIRS
    total = q_blocks * per_block
    width = w_ref.shape[1]
    share = width // 2
    roots = (max(n // 2 - 1, 0), n // 2)

    cache_loads = (
        pltpu.make_async_copy(k_hbm, k_ref, cache_sem.at[0]),
        pltpu.make_async_copy(v_hbm, v_ref, cache_sem.at[1]),
    )

    def load_queries(b):
        return pltpu.make_async_copy(q_hbm.at[b], q_ref.at[b], q_sem.at[b])

    def load_weights(k):
        rows = pl.ds(pl.multiple_of(k * GROUP * HEAD_DIM, GROUP * HEAD_DIM), GROUP * HEAD_DIM)
        return pltpu.make_async_copy(w_hbm.at[rows], w_ref.at[rows], w_sem.at[k])

    load_queries(0).start()
    for load in cache_loads:
        load.start()
    for b in range(1, q_blocks):
        load_queries(b).start()
    for k in range(heads_kv):
        load_weights(k).start()
    acc[...] = jnp.zeros_like(acc)

    barrier = pltpu.get_barrier_semaphore()

    @pl.when(c > 0)
    def _():
        pl.semaphore_signal(barrier, inc=1, device_id={"ctx": c - 1}, device_id_type=MESH)

    @pl.when(c < n - 1)
    def _():
        pl.semaphore_signal(barrier, inc=1, device_id={"ctx": c + 1}, device_id_type=MESH)

    if exchange:
        pl.semaphore_signal(barrier, inc=1, device_id={"head": 1 - h}, device_id_type=MESH)

    for b in range(q_blocks):
        count = jnp.int32(0)
        packed = [jnp.int32(0)] * CAP
        for j in range(pat_ref.shape[1]):
            local = pat_ref[b, j] - c * local_blocks
            inside = (local >= 0) & (local < local_blocks)
            for s in range(CAP):
                packed[s] = jnp.where(inside & (count == s), local, packed[s])
            count = count + inside.astype(jnp.int32)
        for s in range(CAP):
            idx_ref[b, s] = packed[s]
        cnt_ref[b] = count

    pl.semaphore_wait(barrier, (c > 0).astype(jnp.int32) + (c < n - 1).astype(jnp.int32) + int(exchange))

    for load in cache_loads:
        load.wait()

    scale = HEAD_DIM ** (-0.5) * math.log2(math.e)

    def up_copies(u, a, right):
        dst_o, dst_s = (left_o, left_s) if right else (right_o, right_s)
        rec_o, rec_s = (lo_sem, ls_sem) if right else (ro_sem, rs_sem)
        to = {"ctx": c + 1} if right else {"ctx": c - 1}
        return (
            pltpu.make_async_remote_copy(
                send_o.at[u, a], dst_o.at[u, a], so_sem.at[u, a], rec_o.at[u, a],
                device_id=to, device_id_type=MESH),
            pltpu.make_async_remote_copy(
                send_s.at[u, a], dst_s.at[u, a], ss_sem.at[u, a], rec_s.at[u, a],
                device_id=to, device_id_type=MESH),
        )

    def down_copy(u, a, right):
        return pltpu.make_async_remote_copy(
            res.at[u, a], res.at[u, a], (res_right if right else res_left).at[u, a],
            res_recv.at[u, a],
            device_id={"ctx": c + 1} if right else {"ctx": c - 1}, device_id_type=MESH)

    def x_copy(b):
        return pltpu.make_async_remote_copy(
            xs.at[b], xr.at[b], xs_sem.at[b], xr_sem.at[b],
            device_id={"head": 1 - h}, device_id_type=MESH)

    def attend(u):
        b = u // per_block
        k = (u // PAIRS) % heads_kv
        slot = u % slots

        @pl.when(u % per_block == 0)
        def _():
            load_queries(b).wait()

        @pl.when(u % PAIRS == 0)
        def _():
            column = pl.ds(pl.multiple_of(k * HEAD_DIM, HEAD_DIM), HEAD_DIM)
            for s in range(CAP):
                chosen = idx_ref[b, s]
                kg_ref[s * BLOCK:(s + 1) * BLOCK, :] = k_ref[chosen, :, column]
                vg_ref[:, s * BLOCK:(s + 1) * BLOCK] = v_ref[chosen, :, column].T

        count = cnt_ref[b]
        for a in range(2):
            column = pl.multiple_of(((u % per_block) * 2 + a) * UNIT, UNIT)
            q = q_ref[b, :, pl.ds(column, UNIT)]
            q = jnp.concatenate(
                [q[:, i * HEAD_DIM:(i + 1) * HEAD_DIM] for i in range(UNIT_HEADS)], axis=0)
            scores = lax.dot_general(
                kg_ref[...], q, (((1,), (1,)), ((), ())), preferred_element_type=jnp.float32)
            slabs = [scores[s * BLOCK:(s + 1) * BLOCK] for s in range(CAP)]
            top = jnp.full((1, UNIT), NEG, jnp.float32)
            for s, slab in enumerate(slabs):
                peak = jnp.max(slab, axis=0, keepdims=True) * scale
                top = jnp.maximum(top, jnp.where(s < count, peak, NEG))
            weights, norm = [], jnp.zeros((1, UNIT), jnp.float32)
            for s, slab in enumerate(slabs):
                weight = jnp.exp2(slab * scale - jnp.where(s < count, top, -NEG))
                norm = norm + jnp.sum(weight, axis=0, keepdims=True)
                weights.append(weight.astype(jnp.bfloat16))
            own_o[slot, a] = jnp.dot(
                vg_ref[...], jnp.concatenate(weights, axis=0),
                preferred_element_type=jnp.float32)
            for i in range(UNIT_HEADS):
                lanes = slice(i * HEAD_DIM, (i + 1) * HEAD_DIM)
                own_s[slot, a, i:i + 1, :] = top[:, lanes]
                own_s[slot, a, UNIT_HEADS + i:UNIT_HEADS + i + 1, :] = norm[:, lanes]

    def fold(slot, a, got_o, got_s):
        mine = own_s[slot, a]
        m1, l1 = mine[:UNIT_HEADS], mine[UNIT_HEADS:2 * UNIT_HEADS]
        m2, l2 = got_s[:UNIT_HEADS], got_s[UNIT_HEADS:2 * UNIT_HEADS]
        top = jnp.maximum(m1, m2)
        f1, f2 = jnp.exp2(m1 - top), jnp.exp2(m2 - top)
        for i in range(UNIT_HEADS):
            lanes = slice(i * HEAD_DIM, (i + 1) * HEAD_DIM)
            own_o[slot, a, :, lanes] = (
                own_o[slot, a, :, lanes] * f1[i:i + 1]
                + got_o[:, lanes].astype(jnp.float32) * f2[i:i + 1])
        own_s[slot, a, :UNIT_HEADS, :] = top
        own_s[slot, a, UNIT_HEADS:2 * UNIT_HEADS, :] = l1 * f1 + l2 * f2

    def merge(u, a):
        root = roots[a]
        slot = u % slots

        @pl.when((c > 0) & (c <= root))
        def _():
            for copy in up_copies(u, a, True):
                copy.wait_recv()
            fold(slot, a, left_o[u, a], left_s[u, a])

        @pl.when((c < n - 1) & (c >= root))
        def _():
            for copy in up_copies(u, a, False):
                copy.wait_recv()
            fold(slot, a, right_o[u, a], right_s[u, a])

        @pl.when(c != root)
        def _():
            send_o[u, a] = own_o[slot, a].astype(jnp.bfloat16)
            send_s[u, a] = own_s[slot, a]

        @pl.when(c < root)
        def _():
            for copy in up_copies(u, a, True):
                copy.start()

        @pl.when(c > root)
        def _():
            for copy in up_copies(u, a, False):
                copy.start()

        @pl.when(c == root)
        def _():
            norm = own_s[slot, a, UNIT_HEADS:2 * UNIT_HEADS, :]
            for i in range(UNIT_HEADS):
                lanes = slice(i * HEAD_DIM, (i + 1) * HEAD_DIM)
                done = own_o[slot, a, :, lanes] / norm[i:i + 1]
                res[u, a, :, lanes] = done.T.astype(jnp.bfloat16)
            spread(u, a)

    def spread(u, a):
        @pl.when((c > 0) & (c <= roots[a]))
        def _():
            down_copy(u, a, False).start()

        @pl.when((c < n - 1) & (c >= roots[a]))
        def _():
            down_copy(u, a, True).start()

    def receive(u, a):
        @pl.when(c != roots[a])
        def _():
            down_copy(u, a, True).wait_recv()
            spread(u, a)

    def finish(b):
        x_copy(b).wait_recv()
        out_ref[b] = (keep[b] + xr[b].astype(jnp.float32)).astype(out_ref.dtype)

    def project(u):
        b = u // per_block
        k = (u // PAIRS) % heads_kv

        @pl.when(u < per_block)
        def _():
            load_weights(k).wait()

        lhs = jnp.concatenate(
            [res[u - PAIRS + 1 + i, a] for i in range(PAIRS) for a in range(2)], axis=1)
        rows = pl.ds(pl.multiple_of(k * GROUP * HEAD_DIM, GROUP * HEAD_DIM), GROUP * HEAD_DIM)
        tile = min(width, 512)
        for start in range(0, width, tile):
            lanes = slice(start, start + tile)
            acc[:, lanes] += jnp.dot(lhs, w_ref[rows, lanes], preferred_element_type=jnp.float32)

        @pl.when(u % per_block == per_block - 1)
        def _():
            if exchange:
                mine = pl.multiple_of(h * share, 128)
                other = pl.multiple_of((1 - h) * share, 128)
                xs[b] = acc[:, pl.ds(other, share)].astype(jnp.bfloat16)
                x_copy(b).start()
                keep[b] = acc[:, pl.ds(mine, share)]

                @pl.when(b > 0)
                def _():
                    finish(b - 1)
            else:
                out_ref[b] = acc[...]
            acc[...] = jnp.zeros_like(acc)

    def span(far, root):
        return jnp.where(c < root, c, jnp.where(c > root, n - 1 - c, far))

    far = [max(r, n - 1 - r) for r in roots]
    merge_lag = [HOP * span(f, r) for f, r in zip(far, roots)]
    result_lag = [HOP * (f + jnp.abs(c - r)) for f, r in zip(far, roots)]
    last_lag = jnp.maximum(result_lag[0], result_lag[1])
    steps = total + HOP * max(f + max(r, n - 1 - r) for f, r in zip(far, roots))

    def step(t, carry):
        @pl.when(t < total)
        def _():
            attend(t)

        for a in range(2):
            u = t - merge_lag[a]

            @pl.when((u >= 0) & (u < total))
            def _(u=u, a=a):
                merge(u, a)

        for a in range(2):
            u = t - result_lag[a]

            @pl.when((u >= 0) & (u < total))
            def _(u=u, a=a):
                receive(u, a)

        u = t - last_lag

        @pl.when((u >= 0) & (u < total) & (u % PAIRS == PAIRS - 1))
        def _():
            project(u)

        return carry

    lax.fori_loop(0, steps, step, 0)

    if exchange:
        finish(q_blocks - 1)
        for b in range(q_blocks):
            x_copy(b).wait_send()

    def drain(u, carry):
        for a in range(2):
            root = roots[a]

            @pl.when(c != root)
            def _():
                for copy in up_copies(u, a, True):
                    copy.wait_send()

            @pl.when((c > 0) & (c <= root))
            def _():
                down_copy(u, a, False).wait_send()

            @pl.when((c < n - 1) & (c >= root))
            def _():
                down_copy(u, a, True).wait_send()

        return carry

    lax.fori_loop(0, total, drain, 0)


def shards(n, n_head, queries, cached_keys, cached_values, pattern, out_weight):
    query_count, query_width = queries.shape
    q_blocks = query_count // BLOCK
    heads_kv = cached_keys.shape[1] // HEAD_DIM
    total = q_blocks * heads_kv * PAIRS
    width = out_weight.shape[1]
    share = width // 2
    exchange = n_head == 2 and share % 128 == 0
    slots = HOP * (n // 2) + 1
    bf16, f32 = jnp.bfloat16, jnp.float32
    if exchange:
        out_shape = jax.ShapeDtypeStruct((q_blocks, BLOCK, share), bf16)
        x_rows = q_blocks
    else:
        out_shape = jax.ShapeDtypeStruct((q_blocks, BLOCK, width), f32)
        x_rows, share = 1, 128
    units = (total, 2)
    cache_shape = (cached_keys.shape[0] // BLOCK, BLOCK, cached_keys.shape[1])
    sem = pltpu.SemaphoreType.DMA
    any_space = pl.BlockSpec(memory_space=pl.ANY)
    out = pl.pallas_call(
        functools.partial(kernel, n, exchange, slots),
        out_shape=out_shape,
        in_specs=[any_space, any_space, any_space,
                  pl.BlockSpec(memory_space=pltpu.SMEM), any_space],
        out_specs=pl.BlockSpec(memory_space=pltpu.VMEM),
        scratch_shapes=[
            pltpu.VMEM((q_blocks, BLOCK, query_width), bf16),
            pltpu.VMEM(cache_shape, bf16),
            pltpu.VMEM(cache_shape, bf16),
            pltpu.VMEM(out_weight.shape, bf16),
            pltpu.SMEM((q_blocks, CAP), jnp.int32),
            pltpu.SMEM((q_blocks,), jnp.int32),
            pltpu.VMEM((CAP * BLOCK, HEAD_DIM), bf16),
            pltpu.VMEM((HEAD_DIM, CAP * BLOCK), bf16),
            pltpu.VMEM((slots, 2, HEAD_DIM, UNIT), f32),
            pltpu.VMEM((slots, 2, 8, BLOCK), f32),
            pltpu.VMEM(units + (HEAD_DIM, UNIT), bf16),
            pltpu.VMEM(units + (8, BLOCK), f32),
            pltpu.VMEM(units + (HEAD_DIM, UNIT), bf16),
            pltpu.VMEM(units + (8, BLOCK), f32),
            pltpu.VMEM(units + (HEAD_DIM, UNIT), bf16),
            pltpu.VMEM(units + (8, BLOCK), f32),
            pltpu.VMEM(units + (BLOCK, UNIT), bf16),
            pltpu.VMEM((BLOCK, width), f32),
            pltpu.VMEM((x_rows, BLOCK, share), f32),
            pltpu.VMEM((x_rows, BLOCK, share), bf16),
            pltpu.VMEM((x_rows, BLOCK, share), bf16),
            sem((2,)), sem((q_blocks,)), sem((heads_kv,)),
            sem(units), sem(units), sem(units), sem(units), sem(units), sem(units),
            sem(units), sem(units), sem(units),
            sem((x_rows,)), sem((x_rows,)),
        ],
        compiler_params=pltpu.CompilerParams(
            collective_id=0, has_side_effects=True, vmem_limit_bytes=60 * 1024 * 1024),
        cost_estimate=pl.CostEstimate(
            flops=4 * query_count * query_width * CAP * BLOCK
            + 2 * query_count * query_width * width,
            bytes_accessed=2 * (queries.size + 2 * cached_keys.size + out_weight.size),
            transcendentals=query_count * query_width * CAP),
    )(
        queries.reshape(q_blocks, BLOCK, query_width),
        cached_keys.reshape(cache_shape), cached_values.reshape(cache_shape), pattern, out_weight,
    )
    out = out.reshape(query_count, -1)
    if exchange:
        return out
    return lax.psum_scatter(out, "head", scatter_dimension=1, tiled=True).astype(bf16)


def solution(mesh):
    return jax.shard_map(
        functools.partial(shards, mesh.shape["ctx"], mesh.shape["head"]),
        mesh=mesh,
        in_specs=(
            P(("groups", "rep"), "head"),
            P(("groups", "ctx"), "head"),
            P(("groups", "ctx"), "head"),
            P(("groups", "rep"), None),
            P("head", "ctx"),
        ),
        out_specs=P(("groups", "rep"), ("ctx", "head")),
        check_vma=False,
    )
```

```python
import functools
import math

import jax
import jax.numpy as jnp
from jax import lax
from jax.experimental import pallas as pl
from jax.experimental.pallas import tpu as pltpu
from jax.sharding import PartitionSpec as P

HEADS = 64
KV_HEADS = 8
HEAD_DIM = 128
BLOCK = 128
CAP = 8
UNIT_HEADS = 2
GROUP = HEADS // KV_HEADS
PAIRS = GROUP // (2 * UNIT_HEADS)
UNIT = UNIT_HEADS * HEAD_DIM
NEG = -1e30
HOP = 2
MESH = pl.DeviceIdType.MESH


def kernel(n, exchange, slots, q_hbm, k_hbm, v_hbm, pat_ref, w_hbm, out_ref,
           q_ref, k_ref, v_ref, w_ref, idx_ref, cnt_ref, kg_ref, vg_ref,
           own_o, own_s, send_o, send_s, left_o, left_s, right_o, right_s, res,
           acc, keep, xs, xr,
           cache_sem, q_sem, w_sem, so_sem, ss_sem, lo_sem, ls_sem, ro_sem, rs_sem,
           res_recv, res_left, res_right, xs_sem, xr_sem):
    c = lax.axis_index("ctx")
    h = lax.axis_index("head")
    q_blocks = q_ref.shape[0]
    heads_kv = k_ref.shape[2] // HEAD_DIM
    local_blocks = k_ref.shape[0]
    per_block = heads_kv * PAIRS
    total = q_blocks * per_block
    width = w_ref.shape[1]
    share = width // 2
    roots = (max(n // 2 - 1, 0), n // 2)

    cache_loads = (
        pltpu.make_async_copy(k_hbm, k_ref, cache_sem.at[0]),
        pltpu.make_async_copy(v_hbm, v_ref, cache_sem.at[1]),
    )

    def load_queries(b):
        return pltpu.make_async_copy(q_hbm.at[b], q_ref.at[b], q_sem.at[b])

    def load_weights(k):
        rows = pl.ds(pl.multiple_of(k * GROUP * HEAD_DIM, GROUP * HEAD_DIM), GROUP * HEAD_DIM)
        return pltpu.make_async_copy(w_hbm.at[rows], w_ref.at[rows], w_sem.at[k])

    load_queries(0).start()
    for load in cache_loads:
        load.start()
    for b in range(1, q_blocks):
        load_queries(b).start()
    for k in range(heads_kv):
        load_weights(k).start()
    acc[...] = jnp.zeros_like(acc)

    barrier = pltpu.get_barrier_semaphore()

    @pl.when(c > 0)
    def _():
        pl.semaphore_signal(barrier, inc=1, device_id={"ctx": c - 1}, device_id_type=MESH)

    @pl.when(c < n - 1)
    def _():
        pl.semaphore_signal(barrier, inc=1, device_id={"ctx": c + 1}, device_id_type=MESH)

    if exchange:
        pl.semaphore_signal(barrier, inc=1, device_id={"head": 1 - h}, device_id_type=MESH)

    for b in range(q_blocks):
        count = jnp.int32(0)
        packed = [jnp.int32(0)] * CAP
        for j in range(pat_ref.shape[1]):
            local = pat_ref[b, j] - c * local_blocks
            inside = (local >= 0) & (local < local_blocks)
            for s in range(CAP):
                packed[s] = jnp.where(inside & (count == s), local, packed[s])
            count = count + inside.astype(jnp.int32)
        for s in range(CAP):
            idx_ref[b, s] = packed[s]
        cnt_ref[b] = count

    pl.semaphore_wait(barrier, (c > 0).astype(jnp.int32) + (c < n - 1).astype(jnp.int32) + int(exchange))

    for load in cache_loads:
        load.wait()

    scale = HEAD_DIM ** (-0.5) * math.log2(math.e)

    def up_copies(u, a, right):
        dst_o, dst_s = (left_o, left_s) if right else (right_o, right_s)
        rec_o, rec_s = (lo_sem, ls_sem) if right else (ro_sem, rs_sem)
        to = {"ctx": c + 1} if right else {"ctx": c - 1}
        return (
            pltpu.make_async_remote_copy(
                send_o.at[u, a], dst_o.at[u, a], so_sem.at[u, a], rec_o.at[u, a],
                device_id=to, device_id_type=MESH),
            pltpu.make_async_remote_copy(
                send_s.at[u, a], dst_s.at[u, a], ss_sem.at[u, a], rec_s.at[u, a],
                device_id=to, device_id_type=MESH),
        )

    def down_copy(u, a, right):
        return pltpu.make_async_remote_copy(
            res.at[u, a], res.at[u, a], (res_right if right else res_left).at[u, a],
            res_recv.at[u, a],
            device_id={"ctx": c + 1} if right else {"ctx": c - 1}, device_id_type=MESH)

    def x_copy(b):
        return pltpu.make_async_remote_copy(
            xs.at[b], xr.at[b], xs_sem.at[b], xr_sem.at[b],
            device_id={"head": 1 - h}, device_id_type=MESH)

    def prepare(u):
        b = u // per_block
        k = (u // PAIRS) % heads_kv

        @pl.when(u % per_block == 0)
        def _():
            load_queries(b).wait()

        @pl.when(u % PAIRS == 0)
        def _():
            column = pl.ds(pl.multiple_of(k * HEAD_DIM, HEAD_DIM), HEAD_DIM)
            for s in range(CAP):
                chosen = idx_ref[b, s]
                kg_ref[s * BLOCK:(s + 1) * BLOCK, :] = k_ref[chosen, :, column]
                vg_ref[:, s * BLOCK:(s + 1) * BLOCK] = v_ref[chosen, :, column].T

    def attend(u, beside):
        b = u // per_block
        slot = u % slots
        count = cnt_ref[b]
        beside = list(beside)

        def turn():
            if beside:
                beside.pop(0)()

        for a in range(2):
            column = pl.multiple_of(((u % per_block) * 2 + a) * UNIT, UNIT)
            q = q_ref[b, :, pl.ds(column, UNIT)]
            q = jnp.concatenate(
                [q[:, i * HEAD_DIM:(i + 1) * HEAD_DIM] for i in range(UNIT_HEADS)], axis=0)
            scores = lax.dot_general(
                kg_ref[...], q, (((1,), (1,)), ((), ())), preferred_element_type=jnp.float32)
            turn()
            slabs = [scores[s * BLOCK:(s + 1) * BLOCK] for s in range(CAP)]
            top = jnp.full((1, UNIT), NEG, jnp.float32)
            for s, slab in enumerate(slabs):
                peak = jnp.max(slab, axis=0, keepdims=True) * scale
                top = jnp.maximum(top, jnp.where(s < count, peak, NEG))
            weights, norm = [], jnp.zeros((1, UNIT), jnp.float32)
            for s, slab in enumerate(slabs):
                weight = jnp.exp2(slab * scale - jnp.where(s < count, top, -NEG))
                norm = norm + jnp.sum(weight, axis=0, keepdims=True)
                weights.append(weight.astype(jnp.bfloat16))
            turn()
            own_o[slot, a] = jnp.dot(
                vg_ref[...], jnp.concatenate(weights, axis=0),
                preferred_element_type=jnp.float32)
            for i in range(UNIT_HEADS):
                lanes = slice(i * HEAD_DIM, (i + 1) * HEAD_DIM)
                own_s[slot, a, i:i + 1, :] = top[:, lanes]
                own_s[slot, a, UNIT_HEADS + i:UNIT_HEADS + i + 1, :] = norm[:, lanes]
        while beside:
            turn()

    def combine(parts):
        stats = [stat for _, stat in parts]
        tops = [stat[:UNIT_HEADS] for stat in stats]
        top = functools.reduce(jnp.maximum, tops)
        factors = [jnp.exp2(one - top) for one in tops]
        norm = sum(stat[UNIT_HEADS:] * f for stat, f in zip(stats, factors))
        heads = []
        for i in range(UNIT_HEADS):
            lanes = slice(i * HEAD_DIM, (i + 1) * HEAD_DIM)
            heads.append(sum(
                out[:, lanes].astype(jnp.float32) * f[i:i + 1]
                for (out, _), f in zip(parts, factors)))
        return heads, top, norm

    def merge(u, a):
        root = roots[a]
        slot = u % slots

        def arrived(right):
            for copy in up_copies(u, a, right):
                copy.wait_recv()
            if right:
                return left_o[u, a], left_s[u, a]
            return right_o[u, a], right_s[u, a]

        def pass_on(right):
            first = c == 0 if right else c == n - 1

            @pl.when(first)
            def _():
                send_o[u, a] = own_o[slot, a].astype(jnp.bfloat16)
                send_s[u, a] = own_s[slot, a]
                for copy in up_copies(u, a, right):
                    copy.start()

            @pl.when(jnp.logical_not(first))
            def _():
                got = arrived(right)
                heads, top, norm = combine([(own_o[slot, a], own_s[slot, a]), got])
                for i in range(UNIT_HEADS):
                    lanes = slice(i * HEAD_DIM, (i + 1) * HEAD_DIM)
                    send_o[u, a, :, lanes] = heads[i].astype(jnp.bfloat16)
                send_s[u, a, :UNIT_HEADS, :] = top
                send_s[u, a, UNIT_HEADS:, :] = norm
                for copy in up_copies(u, a, right):
                    copy.start()

        @pl.when(c < root)
        def _():
            pass_on(True)

        @pl.when(c > root)
        def _():
            pass_on(False)

        @pl.when(c == root)
        def _():
            parts = [(own_o[slot, a], own_s[slot, a])]
            if root > 0:
                parts.append(arrived(True))
            if root < n - 1:
                parts.append(arrived(False))
            heads, _, norm = combine(parts)
            inverse = 1.0 / norm
            for i in range(UNIT_HEADS):
                lanes = slice(i * HEAD_DIM, (i + 1) * HEAD_DIM)
                res[u, a, :, lanes] = (heads[i] * inverse[i:i + 1]).T.astype(jnp.bfloat16)
            if root > 0:
                down_copy(u, a, False).start()
            if root < n - 1:
                down_copy(u, a, True).start()

    def receive(u, a):
        @pl.when(c != roots[a])
        def _():
            down_copy(u, a, True).wait_recv()

            @pl.when((c > 0) & (c < roots[a]))
            def _():
                down_copy(u, a, False).start()

            @pl.when((c < n - 1) & (c > roots[a]))
            def _():
                down_copy(u, a, True).start()

    def finish(b):
        x_copy(b).wait_recv()
        out_ref[b] = (keep[b] + xr[b].astype(jnp.float32)).astype(out_ref.dtype)

    def await_weights(u):
        @pl.when(u < per_block)
        def _():
            load_weights((u // PAIRS) % heads_kv).wait()

    def project(u):
        k = (u // PAIRS) % heads_kv
        rows = pl.ds(pl.multiple_of(k * GROUP * HEAD_DIM, GROUP * HEAD_DIM), GROUP * HEAD_DIM)
        tile = min(width, 512)

        def one(start):
            lanes = slice(start, start + tile)
            lhs = jnp.concatenate(
                [res[u - PAIRS + 1 + i, a] for i in range(PAIRS) for a in range(2)], axis=1)
            acc[:, lanes] += jnp.dot(lhs, w_ref[rows, lanes], preferred_element_type=jnp.float32)

        return [functools.partial(one, start) for start in range(0, width, tile)]

    def close(u):
        b = u // per_block

        @pl.when(u % per_block == per_block - 1)
        def _():
            if exchange:
                mine = pl.multiple_of(h * share, 128)
                other = pl.multiple_of((1 - h) * share, 128)
                xs[b] = acc[:, pl.ds(other, share)].astype(jnp.bfloat16)
                x_copy(b).start()
                keep[b] = acc[:, pl.ds(mine, share)]

                @pl.when(b > 0)
                def _():
                    finish(b - 1)
            else:
                out_ref[b] = acc[...]
            acc[...] = jnp.zeros_like(acc)

    def span(far, root):
        return jnp.where(c < root, c, jnp.where(c > root, n - 1 - c, far))

    far = [max(r, n - 1 - r) for r in roots]
    merge_lag = [HOP * span(f, r) for f, r in zip(far, roots)]
    result_lag = [HOP * (f + jnp.abs(c - r)) for f, r in zip(far, roots)]
    last_lag = jnp.maximum(result_lag[0], result_lag[1])
    steps = total + 1 + HOP * max(f + max(r, n - 1 - r) for f, r in zip(far, roots))

    def step(t, carry):
        done = t - last_lag - 1
        attending = t < total
        projecting = (done >= 0) & (done < total) & (done % PAIRS == PAIRS - 1)

        @pl.when(attending)
        def _():
            prepare(t)

        @pl.when(projecting)
        def _():
            await_weights(done)

        @pl.when(attending & projecting)
        def _():
            attend(t, project(done))

        @pl.when(attending & jnp.logical_not(projecting))
        def _():
            attend(t, [])

        @pl.when(jnp.logical_not(attending) & projecting)
        def _():
            for one in project(done):
                one()

        for a in range(2):
            u = t - merge_lag[a]

            @pl.when((u >= 0) & (u < total))
            def _(u=u, a=a):
                merge(u, a)

        @pl.when(projecting)
        def _():
            close(done)

        for a in range(2):
            u = t - result_lag[a]

            @pl.when((u >= 0) & (u < total))
            def _(u=u, a=a):
                receive(u, a)

        return carry

    lax.fori_loop(0, steps, step, 0)

    if exchange:
        finish(q_blocks - 1)
        for b in range(q_blocks):
            x_copy(b).wait_send()

    def drain(u, carry):
        for a in range(2):
            root = roots[a]

            @pl.when(c != root)
            def _():
                for copy in up_copies(u, a, True):
                    copy.wait_send()

            @pl.when((c > 0) & (c <= root))
            def _():
                down_copy(u, a, False).wait_send()

            @pl.when((c < n - 1) & (c >= root))
            def _():
                down_copy(u, a, True).wait_send()

        return carry

    lax.fori_loop(0, total, drain, 0)


def shards(n, n_head, queries, cached_keys, cached_values, pattern, out_weight):
    query_count, query_width = queries.shape
    q_blocks = query_count // BLOCK
    heads_kv = cached_keys.shape[1] // HEAD_DIM
    total = q_blocks * heads_kv * PAIRS
    width = out_weight.shape[1]
    share = width // 2
    exchange = n_head == 2 and share % 128 == 0
    slots = HOP * (n // 2) + 1
    bf16, f32 = jnp.bfloat16, jnp.float32
    if exchange:
        out_shape = jax.ShapeDtypeStruct((q_blocks, BLOCK, share), bf16)
        x_rows = q_blocks
    else:
        out_shape = jax.ShapeDtypeStruct((q_blocks, BLOCK, width), f32)
        x_rows, share = 1, 128
    units = (total, 2)
    cache_shape = (cached_keys.shape[0] // BLOCK, BLOCK, cached_keys.shape[1])
    sem = pltpu.SemaphoreType.DMA
    any_space = pl.BlockSpec(memory_space=pl.ANY)
    out = pl.pallas_call(
        functools.partial(kernel, n, exchange, slots),
        out_shape=out_shape,
        in_specs=[any_space, any_space, any_space,
                  pl.BlockSpec(memory_space=pltpu.SMEM), any_space],
        out_specs=pl.BlockSpec(memory_space=pltpu.VMEM),
        scratch_shapes=[
            pltpu.VMEM((q_blocks, BLOCK, query_width), bf16),
            pltpu.VMEM(cache_shape, bf16),
            pltpu.VMEM(cache_shape, bf16),
            pltpu.VMEM(out_weight.shape, bf16),
            pltpu.SMEM((q_blocks, CAP), jnp.int32),
            pltpu.SMEM((q_blocks,), jnp.int32),
            pltpu.VMEM((CAP * BLOCK, HEAD_DIM), bf16),
            pltpu.VMEM((HEAD_DIM, CAP * BLOCK), bf16),
            pltpu.VMEM((slots, 2, HEAD_DIM, UNIT), f32),
            pltpu.VMEM((slots, 2, 2 * UNIT_HEADS, BLOCK), f32),
            pltpu.VMEM(units + (HEAD_DIM, UNIT), bf16),
            pltpu.VMEM(units + (2 * UNIT_HEADS, BLOCK), f32),
            pltpu.VMEM(units + (HEAD_DIM, UNIT), bf16),
            pltpu.VMEM(units + (2 * UNIT_HEADS, BLOCK), f32),
            pltpu.VMEM(units + (HEAD_DIM, UNIT), bf16),
            pltpu.VMEM(units + (2 * UNIT_HEADS, BLOCK), f32),
            pltpu.VMEM(units + (BLOCK, UNIT), bf16),
            pltpu.VMEM((BLOCK, width), f32),
            pltpu.VMEM((x_rows, BLOCK, share), f32),
            pltpu.VMEM((x_rows, BLOCK, share), bf16),
            pltpu.VMEM((x_rows, BLOCK, share), bf16),
            sem((2,)), sem((q_blocks,)), sem((heads_kv,)),
            sem(units), sem(units), sem(units), sem(units), sem(units), sem(units),
            sem(units), sem(units), sem(units),
            sem((x_rows,)), sem((x_rows,)),
        ],
        compiler_params=pltpu.CompilerParams(
            collective_id=0, has_side_effects=True, vmem_limit_bytes=60 * 1024 * 1024),
        cost_estimate=pl.CostEstimate(
            flops=4 * query_count * query_width * CAP * BLOCK
            + 2 * query_count * query_width * width,
            bytes_accessed=2 * (queries.size + 2 * cached_keys.size + out_weight.size),
            transcendentals=query_count * query_width * CAP),
    )(
        queries.reshape(q_blocks, BLOCK, query_width),
        cached_keys.reshape(cache_shape), cached_values.reshape(cache_shape), pattern, out_weight,
    )
    out = out.reshape(query_count, -1)
    if exchange:
        return out
    return lax.psum_scatter(out, "head", scatter_dimension=1, tiled=True).astype(bf16)


def solution(mesh):
    return jax.shard_map(
        functools.partial(shards, mesh.shape["ctx"], mesh.shape["head"]),
        mesh=mesh,
        in_specs=(
            P(("groups", "rep"), "head"),
            P(("groups", "ctx"), "head"),
            P(("groups", "ctx"), "head"),
            P(("groups", "rep"), None),
            P("head", "ctx"),
        ),
        out_specs=P(("groups", "rep"), ("ctx", "head")),
        check_vma=False,
    )
```

```python
import functools
import math

import jax
import jax.numpy as jnp
from jax import lax
from jax.experimental import pallas as pl
from jax.experimental.pallas import tpu as pltpu
from jax.sharding import PartitionSpec as P

HEADS = 64
KV_HEADS = 8
HEAD_DIM = 128
BLOCK = 128
CAP = 8
UNIT_HEADS = 2
GROUP = HEADS // KV_HEADS
PAIRS = GROUP // (2 * UNIT_HEADS)
UNIT = UNIT_HEADS * HEAD_DIM
NEG = -1e30
HOP = 1
MESH = pl.DeviceIdType.MESH


def kernel(n, exchange, slots, q_hbm, k_hbm, v_hbm, pat_ref, w_hbm, out_ref,
           q_ref, k_ref, v_ref, w_ref, idx_ref, cnt_ref, kg_ref, vg_ref,
           own_o, own_s, send_o, send_s, left_o, left_s, right_o, right_s, res,
           acc, keep, xs, xr,
           cache_sem, q_sem, w_sem, so_sem, ss_sem, lo_sem, ls_sem, ro_sem, rs_sem,
           res_recv, res_left, res_right, xs_sem, xr_sem):
    c = lax.axis_index("ctx")
    h = lax.axis_index("head")
    q_blocks = q_ref.shape[0]
    heads_kv = k_ref.shape[2] // HEAD_DIM
    local_blocks = k_ref.shape[0]
    per_block = heads_kv * PAIRS
    total = q_blocks * per_block
    width = w_ref.shape[1]
    share = width // 2
    roots = (max(n // 2 - 1, 0), n // 2)

    cache_loads = (
        pltpu.make_async_copy(k_hbm, k_ref, cache_sem.at[0]),
        pltpu.make_async_copy(v_hbm, v_ref, cache_sem.at[1]),
    )

    def load_queries(b):
        return pltpu.make_async_copy(q_hbm.at[b], q_ref.at[b], q_sem.at[b])

    def load_weights(k):
        rows = pl.ds(pl.multiple_of(k * GROUP * HEAD_DIM, GROUP * HEAD_DIM), GROUP * HEAD_DIM)
        return pltpu.make_async_copy(w_hbm.at[rows], w_ref.at[rows], w_sem.at[k])

    load_queries(0).start()
    for load in cache_loads:
        load.start()
    for b in range(1, q_blocks):
        load_queries(b).start()
    for k in range(heads_kv):
        load_weights(k).start()
    acc[...] = jnp.zeros_like(acc)

    barrier = pltpu.get_barrier_semaphore()

    @pl.when(c > 0)
    def _():
        pl.semaphore_signal(barrier, inc=1, device_id={"ctx": c - 1}, device_id_type=MESH)

    @pl.when(c < n - 1)
    def _():
        pl.semaphore_signal(barrier, inc=1, device_id={"ctx": c + 1}, device_id_type=MESH)

    if exchange:
        pl.semaphore_signal(barrier, inc=1, device_id={"head": 1 - h}, device_id_type=MESH)

    for b in range(q_blocks):
        count = jnp.int32(0)
        packed = [jnp.int32(0)] * CAP
        for j in range(pat_ref.shape[1]):
            local = pat_ref[b, j] - c * local_blocks
            inside = (local >= 0) & (local < local_blocks)
            for s in range(CAP):
                packed[s] = jnp.where(inside & (count == s), local, packed[s])
            count = count + inside.astype(jnp.int32)
        for s in range(CAP):
            idx_ref[b, s] = packed[s]
        cnt_ref[b] = count

    pl.semaphore_wait(barrier, (c > 0).astype(jnp.int32) + (c < n - 1).astype(jnp.int32) + int(exchange))

    for load in cache_loads:
        load.wait()

    scale = HEAD_DIM ** (-0.5) * math.log2(math.e)

    def up_copies(u, a, right):
        dst_o, dst_s = (left_o, left_s) if right else (right_o, right_s)
        rec_o, rec_s = (lo_sem, ls_sem) if right else (ro_sem, rs_sem)
        to = {"ctx": c + 1} if right else {"ctx": c - 1}
        return (
            pltpu.make_async_remote_copy(
                send_o.at[u, a], dst_o.at[u, a], so_sem.at[u, a], rec_o.at[u, a],
                device_id=to, device_id_type=MESH),
            pltpu.make_async_remote_copy(
                send_s.at[u, a], dst_s.at[u, a], ss_sem.at[u, a], rec_s.at[u, a],
                device_id=to, device_id_type=MESH),
        )

    def down_copy(u, a, right):
        return pltpu.make_async_remote_copy(
            res.at[u, a], res.at[u, a], (res_right if right else res_left).at[u, a],
            res_recv.at[u, a],
            device_id={"ctx": c + 1} if right else {"ctx": c - 1}, device_id_type=MESH)

    def x_copy(b):
        return pltpu.make_async_remote_copy(
            xs.at[b], xr.at[b], xs_sem.at[b], xr_sem.at[b],
            device_id={"head": 1 - h}, device_id_type=MESH)

    def prepare(u):
        b = u // per_block
        k = (u // PAIRS) % heads_kv

        @pl.when(u % per_block == 0)
        def _():
            load_queries(b).wait()

        @pl.when(u % PAIRS == 0)
        def _():
            column = pl.ds(pl.multiple_of(k * HEAD_DIM, HEAD_DIM), HEAD_DIM)
            for s in range(CAP):
                chosen = idx_ref[b, s]
                kg_ref[s * BLOCK:(s + 1) * BLOCK, :] = k_ref[chosen, :, column]
                vg_ref[:, s * BLOCK:(s + 1) * BLOCK] = v_ref[chosen, :, column].T

    def attend(u, a, beside):
        b = u // per_block
        slot = u % slots
        count = cnt_ref[b]
        beside = list(beside)

        def turn():
            if beside:
                beside.pop(0)()

        column = pl.multiple_of(((u % per_block) * 2 + a) * UNIT, UNIT)
        q = q_ref[b, :, pl.ds(column, UNIT)]
        q = jnp.concatenate(
            [q[:, i * HEAD_DIM:(i + 1) * HEAD_DIM] for i in range(UNIT_HEADS)], axis=0)
        scores = lax.dot_general(
            kg_ref[...], q, (((1,), (1,)), ((), ())), preferred_element_type=jnp.float32)
        turn()
        slabs = [scores[s * BLOCK:(s + 1) * BLOCK] for s in range(CAP)]
        top = jnp.full((1, UNIT), NEG, jnp.float32)
        for s, slab in enumerate(slabs):
            peak = jnp.max(slab, axis=0, keepdims=True) * scale
            top = jnp.maximum(top, jnp.where(s < count, peak, NEG))
        weights, norm = [], jnp.zeros((1, UNIT), jnp.float32)
        for s, slab in enumerate(slabs):
            weight = jnp.exp2(slab * scale - jnp.where(s < count, top, -NEG))
            norm = norm + jnp.sum(weight, axis=0, keepdims=True)
            weights.append(weight.astype(jnp.bfloat16))
        turn()
        own_o[slot, a] = jnp.dot(
            vg_ref[...], jnp.concatenate(weights, axis=0),
            preferred_element_type=jnp.float32)
        for i in range(UNIT_HEADS):
            lanes = slice(i * HEAD_DIM, (i + 1) * HEAD_DIM)
            own_s[slot, a, i:i + 1, :] = top[:, lanes]
            own_s[slot, a, UNIT_HEADS + i:UNIT_HEADS + i + 1, :] = norm[:, lanes]
        while beside:
            turn()

    def combine(parts):
        stats = [stat for _, stat in parts]
        tops = [stat[:UNIT_HEADS] for stat in stats]
        top = functools.reduce(jnp.maximum, tops)
        factors = [jnp.exp2(one - top) for one in tops]
        norm = sum(stat[UNIT_HEADS:] * f for stat, f in zip(stats, factors))
        heads = []
        for i in range(UNIT_HEADS):
            lanes = slice(i * HEAD_DIM, (i + 1) * HEAD_DIM)
            heads.append(sum(
                out[:, lanes].astype(jnp.float32) * f[i:i + 1]
                for (out, _), f in zip(parts, factors)))
        return heads, top, norm

    def merge(u, a):
        root = roots[a]
        slot = u % slots

        def arrived(right):
            for copy in up_copies(u, a, right):
                copy.wait_recv()
            if right:
                return left_o[u, a], left_s[u, a]
            return right_o[u, a], right_s[u, a]

        def pass_on(right):
            first = c == 0 if right else c == n - 1

            @pl.when(first)
            def _():
                send_o[u, a] = own_o[slot, a].astype(jnp.bfloat16)
                send_s[u, a] = own_s[slot, a]
                for copy in up_copies(u, a, right):
                    copy.start()

            @pl.when(jnp.logical_not(first))
            def _():
                got = arrived(right)
                heads, top, norm = combine([(own_o[slot, a], own_s[slot, a]), got])
                for i in range(UNIT_HEADS):
                    lanes = slice(i * HEAD_DIM, (i + 1) * HEAD_DIM)
                    send_o[u, a, :, lanes] = heads[i].astype(jnp.bfloat16)
                send_s[u, a, :UNIT_HEADS, :] = top
                send_s[u, a, UNIT_HEADS:, :] = norm
                for copy in up_copies(u, a, right):
                    copy.start()

        @pl.when(c < root)
        def _():
            pass_on(True)

        @pl.when(c > root)
        def _():
            pass_on(False)

        @pl.when(c == root)
        def _():
            parts = [(own_o[slot, a], own_s[slot, a])]
            if root > 0:
                parts.append(arrived(True))
            if root < n - 1:
                parts.append(arrived(False))
            heads, _, norm = combine(parts)
            inverse = 1.0 / norm
            for i in range(UNIT_HEADS):
                lanes = slice(i * HEAD_DIM, (i + 1) * HEAD_DIM)
                res[u, a, :, lanes] = (heads[i] * inverse[i:i + 1]).T.astype(jnp.bfloat16)
            if root > 0:
                down_copy(u, a, False).start()
            if root < n - 1:
                down_copy(u, a, True).start()

    def receive(u, a):
        @pl.when(c != roots[a])
        def _():
            down_copy(u, a, True).wait_recv()

            @pl.when((c > 0) & (c < roots[a]))
            def _():
                down_copy(u, a, False).start()

            @pl.when((c < n - 1) & (c > roots[a]))
            def _():
                down_copy(u, a, True).start()

    def finish(b):
        x_copy(b).wait_recv()
        out_ref[b] = (keep[b] + xr[b].astype(jnp.float32)).astype(out_ref.dtype)

    def await_weights(u):
        @pl.when(u < per_block)
        def _():
            load_weights((u // PAIRS) % heads_kv).wait()

    def project(u):
        k = (u // PAIRS) % heads_kv
        rows = pl.ds(pl.multiple_of(k * GROUP * HEAD_DIM, GROUP * HEAD_DIM), GROUP * HEAD_DIM)
        tile = min(width, 512)

        def one(start):
            lanes = slice(start, start + tile)
            lhs = jnp.concatenate(
                [res[u - PAIRS + 1 + i, a] for i in range(PAIRS) for a in range(2)], axis=1)
            acc[:, lanes] += jnp.dot(lhs, w_ref[rows, lanes], preferred_element_type=jnp.float32)

        return [functools.partial(one, start) for start in range(0, width, tile)]

    def close(u):
        b = u // per_block

        @pl.when(u % per_block == per_block - 1)
        def _():
            if exchange:
                mine = pl.multiple_of(h * share, 128)
                other = pl.multiple_of((1 - h) * share, 128)
                xs[b] = acc[:, pl.ds(other, share)].astype(jnp.bfloat16)
                x_copy(b).start()
                keep[b] = acc[:, pl.ds(mine, share)]

                @pl.when(b > 0)
                def _():
                    finish(b - 1)
            else:
                out_ref[b] = acc[...]
            acc[...] = jnp.zeros_like(acc)

    def span(far, root):
        return jnp.where(c < root, c, jnp.where(c > root, n - 1 - c, far))

    far = [max(r, n - 1 - r) for r in roots]
    merge_lag = [HOP * span(f, r) for f, r in zip(far, roots)]
    result_lag = [HOP * (f + jnp.abs(c - r)) for f, r in zip(far, roots)]
    last_lag = jnp.maximum(result_lag[0], result_lag[1])
    steps = total + 1 + HOP * max(f + max(r, n - 1 - r) for f, r in zip(far, roots))

    def step(t, carry):
        done = t - last_lag - 1
        attending = t < total
        projecting = (done >= 0) & (done < total) & (done % PAIRS == PAIRS - 1)

        @pl.when(attending)
        def _():
            prepare(t)

        @pl.when(projecting)
        def _():
            await_weights(done)

        for a in range(2):
            def tiles(a=a):
                tiles = project(done)
                middle = len(tiles) // 2
                return tiles[middle:] if a else tiles[:middle]

            @pl.when(attending & projecting)
            def _(a=a, tiles=tiles):
                attend(t, a, tiles())

            @pl.when(attending & jnp.logical_not(projecting))
            def _(a=a):
                attend(t, a, [])

            @pl.when(jnp.logical_not(attending) & projecting)
            def _(tiles=tiles):
                for one in tiles():
                    one()

            u = t - merge_lag[a]

            @pl.when((u >= 0) & (u < total))
            def _(u=u, a=a):
                merge(u, a)

            if a == 1:
                @pl.when(projecting)
                def _():
                    close(done)

            u = t - result_lag[a]

            @pl.when((u >= 0) & (u < total))
            def _(u=u, a=a):
                receive(u, a)

        return carry

    lax.fori_loop(0, steps, step, 0)

    if exchange:
        finish(q_blocks - 1)
        for b in range(q_blocks):
            x_copy(b).wait_send()

    def drain(u, carry):
        for a in range(2):
            root = roots[a]

            @pl.when(c != root)
            def _():
                for copy in up_copies(u, a, True):
                    copy.wait_send()

            @pl.when((c > 0) & (c <= root))
            def _():
                down_copy(u, a, False).wait_send()

            @pl.when((c < n - 1) & (c >= root))
            def _():
                down_copy(u, a, True).wait_send()

        return carry

    lax.fori_loop(0, total, drain, 0)


def shards(n, n_head, queries, cached_keys, cached_values, pattern, out_weight):
    query_count, query_width = queries.shape
    q_blocks = query_count // BLOCK
    heads_kv = cached_keys.shape[1] // HEAD_DIM
    total = q_blocks * heads_kv * PAIRS
    width = out_weight.shape[1]
    share = width // 2
    exchange = n_head == 2 and share % 128 == 0
    slots = HOP * (n // 2) + 1
    bf16, f32 = jnp.bfloat16, jnp.float32
    if exchange:
        out_shape = jax.ShapeDtypeStruct((q_blocks, BLOCK, share), bf16)
        x_rows = q_blocks
    else:
        out_shape = jax.ShapeDtypeStruct((q_blocks, BLOCK, width), f32)
        x_rows, share = 1, 128
    units = (total, 2)
    cache_shape = (cached_keys.shape[0] // BLOCK, BLOCK, cached_keys.shape[1])
    sem = pltpu.SemaphoreType.DMA
    any_space = pl.BlockSpec(memory_space=pl.ANY)
    out = pl.pallas_call(
        functools.partial(kernel, n, exchange, slots),
        out_shape=out_shape,
        in_specs=[any_space, any_space, any_space,
                  pl.BlockSpec(memory_space=pltpu.SMEM), any_space],
        out_specs=pl.BlockSpec(memory_space=pltpu.VMEM),
        scratch_shapes=[
            pltpu.VMEM((q_blocks, BLOCK, query_width), bf16),
            pltpu.VMEM(cache_shape, bf16),
            pltpu.VMEM(cache_shape, bf16),
            pltpu.VMEM(out_weight.shape, bf16),
            pltpu.SMEM((q_blocks, CAP), jnp.int32),
            pltpu.SMEM((q_blocks,), jnp.int32),
            pltpu.VMEM((CAP * BLOCK, HEAD_DIM), bf16),
            pltpu.VMEM((HEAD_DIM, CAP * BLOCK), bf16),
            pltpu.VMEM((slots, 2, HEAD_DIM, UNIT), f32),
            pltpu.VMEM((slots, 2, 2 * UNIT_HEADS, BLOCK), f32),
            pltpu.VMEM(units + (HEAD_DIM, UNIT), bf16),
            pltpu.VMEM(units + (2 * UNIT_HEADS, BLOCK), f32),
            pltpu.VMEM(units + (HEAD_DIM, UNIT), bf16),
            pltpu.VMEM(units + (2 * UNIT_HEADS, BLOCK), f32),
            pltpu.VMEM(units + (HEAD_DIM, UNIT), bf16),
            pltpu.VMEM(units + (2 * UNIT_HEADS, BLOCK), f32),
            pltpu.VMEM(units + (BLOCK, UNIT), bf16),
            pltpu.VMEM((BLOCK, width), f32),
            pltpu.VMEM((x_rows, BLOCK, share), f32),
            pltpu.VMEM((x_rows, BLOCK, share), bf16),
            pltpu.VMEM((x_rows, BLOCK, share), bf16),
            sem((2,)), sem((q_blocks,)), sem((heads_kv,)),
            sem(units), sem(units), sem(units), sem(units), sem(units), sem(units),
            sem(units), sem(units), sem(units),
            sem((x_rows,)), sem((x_rows,)),
        ],
        compiler_params=pltpu.CompilerParams(
            collective_id=0, has_side_effects=True, vmem_limit_bytes=60 * 1024 * 1024),
        cost_estimate=pl.CostEstimate(
            flops=4 * query_count * query_width * CAP * BLOCK
            + 2 * query_count * query_width * width,
            bytes_accessed=2 * (queries.size + 2 * cached_keys.size + out_weight.size),
            transcendentals=query_count * query_width * CAP),
    )(
        queries.reshape(q_blocks, BLOCK, query_width),
        cached_keys.reshape(cache_shape), cached_values.reshape(cache_shape), pattern, out_weight,
    )
    out = out.reshape(query_count, -1)
    if exchange:
        return out
    return lax.psum_scatter(out, "head", scatter_dimension=1, tiled=True).astype(bf16)


def solution(mesh):
    return jax.shard_map(
        functools.partial(shards, mesh.shape["ctx"], mesh.shape["head"]),
        mesh=mesh,
        in_specs=(
            P(("groups", "rep"), "head"),
            P(("groups", "ctx"), "head"),
            P(("groups", "ctx"), "head"),
            P(("groups", "rep"), None),
            P("head", "ctx"),
        ),
        out_specs=P(("groups", "rep"), ("ctx", "head")),
        check_vma=False,
    )
```

```python
import functools
import math

import jax
import jax.numpy as jnp
from jax import lax
from jax.experimental import pallas as pl
from jax.experimental.pallas import tpu as pltpu
from jax.sharding import PartitionSpec as P

HEADS = 64
KV_HEADS = 8
HEAD_DIM = 128
BLOCK = 128
CAP = 8
UNIT_HEADS = 2
GROUP = HEADS // KV_HEADS
PAIRS = GROUP // (2 * UNIT_HEADS)
UNIT = UNIT_HEADS * HEAD_DIM
NEG = -1e30
HOP = 2
MESH = pl.DeviceIdType.MESH


def kernel(n, exchange, slots, q_hbm, k_hbm, v_hbm, pat_ref, w_hbm, out_ref,
           q_ref, k_ref, v_ref, w_ref, idx_ref, cnt_ref, kg_ref, vg_ref,
           own_o, own_s, send_o, send_s, left_o, left_s, right_o, right_s, res,
           acc, keep, xs, xr,
           cache_sem, q_sem, w_sem, so_sem, ss_sem, lo_sem, ls_sem, ro_sem, rs_sem,
           res_recv, res_left, res_right, xs_sem, xr_sem):
    c = lax.axis_index("ctx")
    h = lax.axis_index("head")
    q_blocks = q_ref.shape[0]
    heads_kv = k_ref.shape[2] // HEAD_DIM
    local_blocks = k_ref.shape[0]
    per_block = heads_kv * PAIRS
    total = q_blocks * per_block
    width = w_ref.shape[1]
    share = width // 2
    roots = (max(n // 2 - 1, 0), n // 2)

    cache_loads = (
        pltpu.make_async_copy(k_hbm, k_ref, cache_sem.at[0]),
        pltpu.make_async_copy(v_hbm, v_ref, cache_sem.at[1]),
    )

    def load_queries(b):
        return pltpu.make_async_copy(q_hbm.at[b], q_ref.at[b], q_sem.at[b])

    def load_weights(k):
        rows = pl.ds(pl.multiple_of(k * GROUP * HEAD_DIM, GROUP * HEAD_DIM), GROUP * HEAD_DIM)
        return pltpu.make_async_copy(w_hbm.at[rows], w_ref.at[rows], w_sem.at[k])

    load_queries(0).start()
    for load in cache_loads:
        load.start()
    for b in range(1, q_blocks):
        load_queries(b).start()
    for k in range(heads_kv):
        load_weights(k).start()
    acc[...] = jnp.zeros_like(acc)

    barrier = pltpu.get_barrier_semaphore()

    @pl.when(c > 0)
    def _():
        pl.semaphore_signal(barrier, inc=1, device_id={"ctx": c - 1}, device_id_type=MESH)

    @pl.when(c < n - 1)
    def _():
        pl.semaphore_signal(barrier, inc=1, device_id={"ctx": c + 1}, device_id_type=MESH)

    if exchange:
        pl.semaphore_signal(barrier, inc=1, device_id={"head": 1 - h}, device_id_type=MESH)

    for b in range(q_blocks):
        count = jnp.int32(0)
        packed = [jnp.int32(0)] * CAP
        for j in range(pat_ref.shape[1]):
            local = pat_ref[b, j] - c * local_blocks
            inside = (local >= 0) & (local < local_blocks)
            for s in range(CAP):
                packed[s] = jnp.where(inside & (count == s), local, packed[s])
            count = count + inside.astype(jnp.int32)
        for s in range(CAP):
            idx_ref[b, s] = packed[s]
        cnt_ref[b] = count

    pl.semaphore_wait(barrier, (c > 0).astype(jnp.int32) + (c < n - 1).astype(jnp.int32) + int(exchange))

    for load in cache_loads:
        load.wait()

    scale = HEAD_DIM ** (-0.5) * math.log2(math.e)

    def up_copies(u, a, right):
        dst_o, dst_s = (left_o, left_s) if right else (right_o, right_s)
        rec_o, rec_s = (lo_sem, ls_sem) if right else (ro_sem, rs_sem)
        to = {"ctx": c + 1} if right else {"ctx": c - 1}
        return (
            pltpu.make_async_remote_copy(
                send_o.at[u, a], dst_o.at[u, a], so_sem.at[u, a], rec_o.at[u, a],
                device_id=to, device_id_type=MESH),
            pltpu.make_async_remote_copy(
                send_s.at[u, a], dst_s.at[u, a], ss_sem.at[u, a], rec_s.at[u, a],
                device_id=to, device_id_type=MESH),
        )

    def down_copy(u, a, right):
        return pltpu.make_async_remote_copy(
            res.at[u, a], res.at[u, a], (res_right if right else res_left).at[u, a],
            res_recv.at[u, a],
            device_id={"ctx": c + 1} if right else {"ctx": c - 1}, device_id_type=MESH)

    def x_copy(b):
        return pltpu.make_async_remote_copy(
            xs.at[b], xr.at[b], xs_sem.at[b], xr_sem.at[b],
            device_id={"head": 1 - h}, device_id_type=MESH)

    def prepare(u):
        b = u // per_block
        k = (u // PAIRS) % heads_kv

        @pl.when(u % per_block == 0)
        def _():
            load_queries(b).wait()

        @pl.when(u % PAIRS == 0)
        def _():
            column = pl.ds(pl.multiple_of(k * HEAD_DIM, HEAD_DIM), HEAD_DIM)
            for s in range(CAP):
                chosen = idx_ref[b, s]
                kg_ref[s * BLOCK:(s + 1) * BLOCK, :] = k_ref[chosen, :, column]
                vg_ref[:, s * BLOCK:(s + 1) * BLOCK] = v_ref[chosen, :, column].T

    def attend(u, a, beside):
        b = u // per_block
        slot = u % slots
        count = cnt_ref[b]
        beside = list(beside)

        def turn():
            if beside:
                beside.pop(0)()

        column = pl.multiple_of(((u % per_block) * 2 + a) * UNIT, UNIT)
        q = q_ref[b, :, pl.ds(column, UNIT)]
        q = jnp.concatenate(
            [q[:, i * HEAD_DIM:(i + 1) * HEAD_DIM] for i in range(UNIT_HEADS)], axis=0)
        scores = lax.dot_general(
            kg_ref[...], q, (((1,), (1,)), ((), ())), preferred_element_type=jnp.float32)
        turn()
        slabs = [scores[s * BLOCK:(s + 1) * BLOCK] for s in range(CAP)]
        top = jnp.full((1, UNIT), NEG, jnp.float32)
        for s, slab in enumerate(slabs):
            peak = jnp.max(slab, axis=0, keepdims=True) * scale
            top = jnp.maximum(top, jnp.where(s < count, peak, NEG))
        weights, norm = [], jnp.zeros((1, UNIT), jnp.float32)
        for s, slab in enumerate(slabs):
            weight = jnp.exp2(slab * scale - jnp.where(s < count, top, -NEG))
            norm = norm + jnp.sum(weight, axis=0, keepdims=True)
            weights.append(weight.astype(jnp.bfloat16))
        turn()
        own_o[slot, a] = jnp.dot(
            vg_ref[...], jnp.concatenate(weights, axis=0),
            preferred_element_type=jnp.float32)
        for i in range(UNIT_HEADS):
            lanes = slice(i * HEAD_DIM, (i + 1) * HEAD_DIM)
            own_s[slot, a, i:i + 1, :] = top[:, lanes]
            own_s[slot, a, UNIT_HEADS + i:UNIT_HEADS + i + 1, :] = norm[:, lanes]
        while beside:
            turn()

    def combine(parts):
        stats = [stat for _, stat in parts]
        tops = [stat[:UNIT_HEADS] for stat in stats]
        top = functools.reduce(jnp.maximum, tops)
        factors = [jnp.exp2(one - top) for one in tops]
        norm = sum(stat[UNIT_HEADS:] * f for stat, f in zip(stats, factors))
        heads = []
        for i in range(UNIT_HEADS):
            lanes = slice(i * HEAD_DIM, (i + 1) * HEAD_DIM)
            heads.append(sum(
                out[:, lanes].astype(jnp.float32) * f[i:i + 1]
                for (out, _), f in zip(parts, factors)))
        return heads, top, norm

    def merge(u, a):
        root = roots[a]
        slot = u % slots

        def arrived(right):
            for copy in up_copies(u, a, right):
                copy.wait_recv()
            if right:
                return left_o[u, a], left_s[u, a]
            return right_o[u, a], right_s[u, a]

        def pass_on(right):
            first = c == 0 if right else c == n - 1

            @pl.when(first)
            def _():
                send_o[u, a] = own_o[slot, a].astype(jnp.bfloat16)
                send_s[u, a] = own_s[slot, a]
                for copy in up_copies(u, a, right):
                    copy.start()

            @pl.when(jnp.logical_not(first))
            def _():
                got = arrived(right)
                heads, top, norm = combine([(own_o[slot, a], own_s[slot, a]), got])
                for i in range(UNIT_HEADS):
                    lanes = slice(i * HEAD_DIM, (i + 1) * HEAD_DIM)
                    send_o[u, a, :, lanes] = heads[i].astype(jnp.bfloat16)
                send_s[u, a, :UNIT_HEADS, :] = top
                send_s[u, a, UNIT_HEADS:, :] = norm
                for copy in up_copies(u, a, right):
                    copy.start()

        @pl.when(c < root)
        def _():
            pass_on(True)

        @pl.when(c > root)
        def _():
            pass_on(False)

        @pl.when(c == root)
        def _():
            parts = [(own_o[slot, a], own_s[slot, a])]
            if root > 0:
                parts.append(arrived(True))
            if root < n - 1:
                parts.append(arrived(False))
            heads, _, norm = combine(parts)
            inverse = 1.0 / norm
            for i in range(UNIT_HEADS):
                lanes = slice(i * HEAD_DIM, (i + 1) * HEAD_DIM)
                res[u, a, :, lanes] = (heads[i] * inverse[i:i + 1]).T.astype(jnp.bfloat16)
            if root > 0:
                down_copy(u, a, False).start()
            if root < n - 1:
                down_copy(u, a, True).start()

    def receive(u, a):
        @pl.when(c != roots[a])
        def _():
            down_copy(u, a, True).wait_recv()

            @pl.when((c > 0) & (c < roots[a]))
            def _():
                down_copy(u, a, False).start()

            @pl.when((c < n - 1) & (c > roots[a]))
            def _():
                down_copy(u, a, True).start()

    def finish(b):
        x_copy(b).wait_recv()
        out_ref[b] = (keep[b] + xr[b].astype(jnp.float32)).astype(out_ref.dtype)

    def await_weights(u):
        @pl.when(u < per_block)
        def _():
            load_weights((u // PAIRS) % heads_kv).wait()

    def project(u):
        k = (u // PAIRS) % heads_kv
        rows = pl.ds(pl.multiple_of(k * GROUP * HEAD_DIM, GROUP * HEAD_DIM), GROUP * HEAD_DIM)
        tile = min(width, 512)

        def one(start):
            lanes = slice(start, start + tile)
            lhs = jnp.concatenate(
                [res[u - PAIRS + 1 + i, a] for i in range(PAIRS) for a in range(2)], axis=1)
            acc[:, lanes] += jnp.dot(lhs, w_ref[rows, lanes], preferred_element_type=jnp.float32)

        return [functools.partial(one, start) for start in range(0, width, tile)]

    def close(u):
        b = u // per_block

        @pl.when(u % per_block == per_block - 1)
        def _():
            if exchange:
                mine = pl.multiple_of(h * share, 128)
                other = pl.multiple_of((1 - h) * share, 128)
                xs[b] = acc[:, pl.ds(other, share)].astype(jnp.bfloat16)
                x_copy(b).start()
                keep[b] = acc[:, pl.ds(mine, share)]

                @pl.when(b > 0)
                def _():
                    finish(b - 1)
            else:
                out_ref[b] = acc[...]
            acc[...] = jnp.zeros_like(acc)

    def span(far, root):
        return jnp.where(c < root, c, jnp.where(c > root, n - 1 - c, far))

    far = [max(r, n - 1 - r) for r in roots]
    merge_lag = [HOP * span(f, r) for f, r in zip(far, roots)]
    result_lag = [HOP * (f + jnp.abs(c - r)) for f, r in zip(far, roots)]
    last_lag = jnp.maximum(result_lag[0], result_lag[1])
    steps = total + 1 + HOP * max(f + max(r, n - 1 - r) for f, r in zip(far, roots))

    def step(t, carry):
        done = t - last_lag - 1
        attending = t < total
        projecting = (done >= 0) & (done < total) & (done % PAIRS == PAIRS - 1)

        @pl.when(attending)
        def _():
            prepare(t)

        @pl.when(projecting)
        def _():
            await_weights(done)

        for a in range(2):
            def tiles(a=a):
                tiles = project(done)
                middle = len(tiles) // 2
                return tiles[middle:] if a else tiles[:middle]

            @pl.when(attending & projecting)
            def _(a=a, tiles=tiles):
                attend(t, a, tiles())

            @pl.when(attending & jnp.logical_not(projecting))
            def _(a=a):
                attend(t, a, [])

            @pl.when(jnp.logical_not(attending) & projecting)
            def _(tiles=tiles):
                for one in tiles():
                    one()

            u = t - merge_lag[a]

            @pl.when((u >= 0) & (u < total))
            def _(u=u, a=a):
                merge(u, a)

            if a == 1:
                @pl.when(projecting)
                def _():
                    close(done)

            u = t - result_lag[a]

            @pl.when((u >= 0) & (u < total))
            def _(u=u, a=a):
                receive(u, a)

        return carry

    lax.fori_loop(0, steps, step, 0)

    if exchange:
        finish(q_blocks - 1)
        for b in range(q_blocks):
            x_copy(b).wait_send()

    def drain(u, carry):
        for a in range(2):
            root = roots[a]

            @pl.when(c != root)
            def _():
                for copy in up_copies(u, a, True):
                    copy.wait_send()

            @pl.when((c > 0) & (c <= root))
            def _():
                down_copy(u, a, False).wait_send()

            @pl.when((c < n - 1) & (c >= root))
            def _():
                down_copy(u, a, True).wait_send()

        return carry

    lax.fori_loop(0, total, drain, 0)


def shards(n, n_head, queries, cached_keys, cached_values, pattern, out_weight):
    query_count, query_width = queries.shape
    q_blocks = query_count // BLOCK
    heads_kv = cached_keys.shape[1] // HEAD_DIM
    total = q_blocks * heads_kv * PAIRS
    width = out_weight.shape[1]
    share = width // 2
    exchange = n_head == 2 and share % 128 == 0
    slots = HOP * (n // 2) + 1
    bf16, f32 = jnp.bfloat16, jnp.float32
    if exchange:
        out_shape = jax.ShapeDtypeStruct((q_blocks, BLOCK, share), bf16)
        x_rows = q_blocks
    else:
        out_shape = jax.ShapeDtypeStruct((q_blocks, BLOCK, width), f32)
        x_rows, share = 1, 128
    units = (total, 2)
    cache_shape = (cached_keys.shape[0] // BLOCK, BLOCK, cached_keys.shape[1])
    sem = pltpu.SemaphoreType.DMA
    any_space = pl.BlockSpec(memory_space=pl.ANY)
    out = pl.pallas_call(
        functools.partial(kernel, n, exchange, slots),
        out_shape=out_shape,
        in_specs=[any_space, any_space, any_space,
                  pl.BlockSpec(memory_space=pltpu.SMEM), any_space],
        out_specs=pl.BlockSpec(memory_space=pltpu.VMEM),
        scratch_shapes=[
            pltpu.VMEM((q_blocks, BLOCK, query_width), bf16),
            pltpu.VMEM(cache_shape, bf16),
            pltpu.VMEM(cache_shape, bf16),
            pltpu.VMEM(out_weight.shape, bf16),
            pltpu.SMEM((q_blocks, CAP), jnp.int32),
            pltpu.SMEM((q_blocks,), jnp.int32),
            pltpu.VMEM((CAP * BLOCK, HEAD_DIM), bf16),
            pltpu.VMEM((HEAD_DIM, CAP * BLOCK), bf16),
            pltpu.VMEM((slots, 2, HEAD_DIM, UNIT), f32),
            pltpu.VMEM((slots, 2, 2 * UNIT_HEADS, BLOCK), f32),
            pltpu.VMEM(units + (HEAD_DIM, UNIT), bf16),
            pltpu.VMEM(units + (2 * UNIT_HEADS, BLOCK), f32),
            pltpu.VMEM(units + (HEAD_DIM, UNIT), bf16),
            pltpu.VMEM(units + (2 * UNIT_HEADS, BLOCK), f32),
            pltpu.VMEM(units + (HEAD_DIM, UNIT), bf16),
            pltpu.VMEM(units + (2 * UNIT_HEADS, BLOCK), f32),
            pltpu.VMEM(units + (BLOCK, UNIT), bf16),
            pltpu.VMEM((BLOCK, width), f32),
            pltpu.VMEM((x_rows, BLOCK, share), f32),
            pltpu.VMEM((x_rows, BLOCK, share), bf16),
            pltpu.VMEM((x_rows, BLOCK, share), bf16),
            sem((2,)), sem((q_blocks,)), sem((heads_kv,)),
            sem(units), sem(units), sem(units), sem(units), sem(units), sem(units),
            sem(units), sem(units), sem(units),
            sem((x_rows,)), sem((x_rows,)),
        ],
        compiler_params=pltpu.CompilerParams(
            collective_id=0, has_side_effects=True, vmem_limit_bytes=60 * 1024 * 1024),
        cost_estimate=pl.CostEstimate(
            flops=4 * query_count * query_width * CAP * BLOCK
            + 2 * query_count * query_width * width,
            bytes_accessed=2 * (queries.size + 2 * cached_keys.size + out_weight.size),
            transcendentals=query_count * query_width * CAP),
    )(
        queries.reshape(q_blocks, BLOCK, query_width),
        cached_keys.reshape(cache_shape), cached_values.reshape(cache_shape), pattern, out_weight,
    )
    out = out.reshape(query_count, -1)
    if exchange:
        return out
    return lax.psum_scatter(out, "head", scatter_dimension=1, tiled=True).astype(bf16)


def solution(mesh):
    return jax.shard_map(
        functools.partial(shards, mesh.shape["ctx"], mesh.shape["head"]),
        mesh=mesh,
        in_specs=(
            P(("groups", "rep"), "head"),
            P(("groups", "ctx"), "head"),
            P(("groups", "ctx"), "head"),
            P(("groups", "rep"), None),
            P("head", "ctx"),
        ),
        out_specs=P(("groups", "rep"), ("ctx", "head")),
        check_vma=False,
    )
```
